32 devices in a mesh: groups: 2 (over y), pool: 4 (over z), tp: 4 (over x, core).
Axes of the slice: x: 2, y: 2, z: 4, core: 2. Of those that a mesh axis runs over, the one named last changes fastest.
Arguments:
- tokens: bfloat16 [3072, 5120], P(('groups', 'pool'), 'tp'), parts along dimension 0, may hold values from -16 to 16
- query_matrix: bfloat16 [5120, 4096], P('pool', 'tp'), may hold values from -0.078125 to 0.078125
- key_matrix: bfloat16 [5120, 1024], P('pool', 'tp'), may hold values from -0.078125 to 0.078125
- value_matrix: bfloat16 [5120, 1024], P('pool', 'tp'), may hold values from -0.078125 to 0.078125
- query_down_maps: bfloat16 [16, 5120, 64], P(('groups', 'pool'), 'tp'), parts along dimension 0, may hold values from -0.078125 to 0.078125
- query_up_maps: bfloat16 [16, 64, 4096], P(('groups', 'pool'), None, 'tp'), parts along dimension 0, may hold values from -0.75 to 0.75
- request_lengths: int32 [8, 48], P(('groups', 'pool')), parts along dimension 0, may hold values from 1 to 16, 384 in all within a row
- request_adapter: int32 [384, 1], P(('groups', 'pool')), parts along dimension 0, may hold values from 0 to 7; in each aligned block of 48 rows (0 to 47, 48 to 95, ...) at most 6 rows name the same one
- adapter_pool_slot: int32 [8], replicated, may hold values from 0 to 7, each once
Outputs:
- mixed: bfloat16 [3072, 4096], P(('groups', 'pool'), 'tp'), parts along dimension 0
The draws below stay inside these ranges and needn't reach their ends.
There are 2 independent parts, one for each index of `groups`. The reference program is written for one: setup_inputs(seed, part) draws one part's arguments, and reference() takes and returns one part's arrays. A program takes and returns all parts, laid end to end along the dimension named above; an argument that names none is the same for every part. Nothing has to cross between parts.
Inputs may be any that keep to these rules, and one draw needn't show every extreme that they name: `request_lengths`: each pool device's 48 requests cover its 384 tokens; some request has exactly 16 tokens. `request_adapter`: the requests of one pool device name one adapter at most 6 times, and this is reached; every adapter is named. A permutation: adapter a is stored at slot adapter_pool_slot[a]; slot s lies on the pool device of index floor(s / 2).
All inputs are finite; a program needn't handle non-finite values.
Results may differ from the reference program's by a relative error of at most 0.012.
The reference program's roundings to bfloat16 on the way (of `low_rank`, `delta`, `queries` and `softmax_w`) count: a program that leaves them out, or rounds other values in their place, can miss the bound.
Values may be sent and summed in bfloat16 or wider, within the bound.
No kernel may reach another device: no remote copies, remote signals or barrier semaphores. Data moves between devices by JAX's collectives and lax.ppermute only.
A program may use at most 128 MiB of HBM per device.

```python
import math
import jax
import jax.numpy as jnp
import numpy as np
from jax import lax

MODEL_WIDTH = 5120
HEADS = 32
KV_HEADS = 8
HEAD_DIM = 128
ADAPTER_RANK = 64
TOK_DEV = 384
LEN_MOST = 16
QUERY_WIDTH = 4096
KW = 1024
REQS_DEV = 48
POOL_ADAPTERS = 8
SAME_MOST = 6
TOKENS = 1536
REQUESTS = 192
N_POOL = 4


def draw_tokens(key, part):
    key = jax.random.fold_in(key, 11)
    return jnp.clip(jax.random.normal(key, (TOKENS, MODEL_WIDTH), jnp.float32), -6.0, 6.0).astype(jnp.bfloat16)


def steps_of(stream_key, shape, pieces, smallest, high):
    def one(dim, blocks):
        draws = jax.random.uniform(jax.random.fold_in(jax.random.fold_in(stream_key, 6), dim), (blocks,), jnp.float32, smallest / len(pieces), high / len(pieces))
        return jnp.repeat(jnp.exp(draws), shape[dim] // blocks).reshape((-1,) + (1,) * (len(shape) - dim - 1))

    loudness = one(*pieces[0])
    for cut in pieces[1:]:
        loudness = loudness * one(*cut)
    return loudness


def length_profile(amount, total, bound, slope):
    portions = [(1 << 20) // math.isqrt(rank ** slope) + 1 for rank in range(2, amount + 1)]
    rest, given = total - bound - (amount - 1), [1] * (amount - 1)
    while rest > 0:
        movable = [i for i in range(amount - 1) if given[i] < bound]
        pool, budget = sum([portions[i] for i in movable]), rest
        for i in movable:
            addition = min(bound - given[i], max(1, budget * portions[i] // pool), rest)
            given[i] = given[i] + addition
            rest = rest - addition
    return np.array([bound] + given)


def uneven(stream_key, number_of, total, bound, lean):
    if number_of == 2:
        one = jax.random.randint(stream_key, (), max(1, total - bound), min(bound, total - 1) + 1)
        return jnp.stack([one, total - one])
    lengths = jnp.asarray(length_profile(number_of, total, bound, lean), jnp.int32)
    couples = (number_of - 1) // 2
    source_of, sink = lengths[1:1 + 2 * couples:2], lengths[2:2 + 2 * couples:2]
    slack = jnp.minimum(source_of - 1, bound - sink)
    moved = jax.random.randint(jax.random.fold_in(stream_key, 1), (couples,), 0, 1 << 20) % (slack + 1)
    lengths = lengths.at[1:1 + 2 * couples:2].set(source_of - moved).at[2:2 + 2 * couples:2].set(sink + moved)
    return lengths[jax.random.permutation(jax.random.fold_in(stream_key, 2), number_of)]


def deal_out(stream_key, own, number, rows, amount, top, bound, lean):
    ranking = jax.random.permutation(stream_key, amount)
    packed, ordinary = shares(amount, rows * top, bound, lean, True), shares(amount, rows * top, bound, lean, False)
    places = jnp.arange(amount)

    def named(sizes, turn):
        used = int((sizes > 0).sum())
        fixed = max(1, used // 4)
        moved = fixed + (places - fixed + turn * (used - fixed)) % max(1, amount - fixed)
        return jnp.zeros((amount,), jnp.int32).at[ranking[jnp.where(places < fixed, places, moved)]].set(jnp.asarray(sizes, jnp.int32))

    sizes = jnp.where(number % 4 == 0, named(packed, number // 4), named(ordinary, number - number // 4 - 1))
    mixed = jax.random.permutation(jax.random.fold_in(own, 3), amount)
    donor, receiver = mixed[0:amount // 2 * 2:2], mixed[1:amount // 2 * 2:2]
    slack = jnp.minimum(sizes[donor] - 1, bound - sizes[receiver]) // 2
    slack = jnp.where((donor == ranking[0]) | (receiver == ranking[0]) | (sizes[receiver] == 0), 0, jnp.maximum(slack, 0))
    moved = jax.random.randint(jax.random.fold_in(own, 4), (amount // 2,), 0, 1 << 20) % (slack + 1)
    sizes = sizes.at[donor].add(-moved).at[receiver].add(moved)
    labels = jnp.searchsorted(jnp.cumsum(sizes), jnp.arange(rows * top), side="right").astype(jnp.int32)
    table = labels.reshape(top, rows).T
    table = table[jax.random.permutation(jax.random.fold_in(own, 1), rows)]
    turn = jax.random.randint(jax.random.fold_in(own, 2), (rows, 1), 0, top)
    return jnp.take_along_axis(table, (jnp.arange(top)[None, :] + turn) % top, axis=1)


def shares(amount, total, most, lean, full):
    weights = [(1 << 20) // math.isqrt(standing ** lean) + 1 for standing in range(1, amount + 1)]
    largest = most if full else min(most, max(-(-total // amount), total * weights[0] // sum(weights)))
    least = 1 if total - largest >= amount - 1 else 0
    counts, surplus = [largest] + [least] * (amount - 1), total - largest - least * (amount - 1)
    while surplus > 0:
        candidates = [i for i in range(1, amount) if counts[i] < largest] or [i for i in range(1, amount) if counts[i] < most]
        whole, left = sum([weights[i] for i in candidates]), surplus
        for i in candidates:
            more = min(most - counts[i], max(1, left * weights[i] // whole), surplus)
            counts[i] = counts[i] + more
            surplus = surplus - more
    return np.array(counts)


def noise(key, dims, scale, limit, cuts=(), kind=jnp.bfloat16):
    array = jax.random.normal(key, dims, jnp.float32) * scale
    if len(cuts) > 0:
        array = steps_of(key, dims, cuts, -0.22, 0.18) * array
    return jnp.clip(array, min=-limit, max=limit).astype(kind)


def setup_inputs(seed: int = 0, part: int = 0) -> dict:
    streams_of = jax.random.split(jax.random.key(seed), 10)
    part_keys = jax.random.split(jax.random.fold_in(streams_of[9], part), 10)
    tokens = draw_tokens(jax.random.fold_in(jax.random.fold_in(streams_of[9], part), 71), part)
    query_matrix = noise(streams_of[1], (MODEL_WIDTH, QUERY_WIDTH), MODEL_WIDTH ** -0.5, 0.078125, ((0, 4), (1, 4)))
    key_matrix = noise(streams_of[2], (MODEL_WIDTH, KW), MODEL_WIDTH ** -0.5, 0.078125, ((0, 4), (1, 4)))
    value_matrix = noise(streams_of[3], (MODEL_WIDTH, KW), MODEL_WIDTH ** -0.5, 0.078125, ((0, 4), (1, 4)))
    query_down_maps = noise(part_keys[4], (POOL_ADAPTERS, MODEL_WIDTH, ADAPTER_RANK), MODEL_WIDTH ** -0.5, 0.078125, ((0, 4), (1, 4)))
    query_up_maps = noise(part_keys[5], (POOL_ADAPTERS, ADAPTER_RANK, QUERY_WIDTH), ADAPTER_RANK ** -0.5, 0.75, ((0, 4), (2, 4)))
    request_lengths = jax.vmap(lambda own: uneven(own, REQS_DEV, TOK_DEV, LEN_MOST, 2))(jax.random.split(part_keys[6], N_POOL)).reshape((N_POOL, REQS_DEV)).astype(jnp.int32)
    request_adapter_keys = jax.random.split(jax.random.fold_in(part_keys[7], 1), REQUESTS // REQS_DEV)
    request_adapter_turns = jax.random.permutation(jax.random.fold_in(part_keys[7], 3), REQUESTS // REQS_DEV)
    request_adapter = jax.vmap(lambda own, number: deal_out(jax.random.fold_in(part_keys[7], 2), own, number, REQS_DEV, POOL_ADAPTERS, 1, SAME_MOST, 2))(request_adapter_keys, request_adapter_turns).reshape((REQUESTS, 1))
    adapter_pool_slot = jax.random.permutation(streams_of[8], POOL_ADAPTERS).astype(jnp.int32)
    return {"tokens": tokens, "query_matrix": query_matrix, "key_matrix": key_matrix, "value_matrix": value_matrix, "query_down_maps": query_down_maps, "query_up_maps": query_up_maps, "request_lengths": request_lengths, "request_adapter": request_adapter, "adapter_pool_slot": adapter_pool_slot}


def request_local(request_lengths):
    boundary = jnp.cumsum(request_lengths, axis=1, dtype=jnp.int32)
    position = jnp.arange(TOK_DEV, dtype=jnp.int32)
    return jnp.sum((position[None, :, None] >= boundary[:, None, :]).astype(jnp.int32), axis=2, dtype=jnp.int32)


def attend_block(query_blk, key_blk, value_blk, request):
    group_size = HEADS // KV_HEADS
    query_h = query_blk.reshape(TOK_DEV, KV_HEADS, group_size, HEAD_DIM).astype(jnp.float32)
    key_h = key_blk.reshape(TOK_DEV, KV_HEADS, HEAD_DIM).astype(jnp.float32)
    value_h = value_blk.reshape(TOK_DEV, KV_HEADS, HEAD_DIM).astype(jnp.float32)
    scores = jnp.einsum("tkgd,skd->kgts", query_h, key_h) * (HEAD_DIM ** -0.5)
    position = jnp.arange(TOK_DEV)
    allowed = (request[:, None] == request[None, :]) & (position[None, :] <= position[:, None])
    scores = jnp.where(allowed, scores, -1e30)
    top_score = jnp.max(scores, axis=-1, keepdims=True)
    exp_terms = jnp.exp(scores - top_score)
    softmax_w = (exp_terms / jnp.sum(exp_terms, axis=-1, keepdims=True)).astype(jnp.bfloat16)
    mixed = jnp.einsum("kgts,skd->tkgd", softmax_w.astype(jnp.float32), value_h)
    return mixed.astype(jnp.bfloat16).reshape(TOK_DEV, QUERY_WIDTH)


def reference(tokens, query_matrix, key_matrix, value_matrix, query_down_maps, query_up_maps, request_lengths, request_adapter, adapter_pool_slot):
    local = request_local(request_lengths)
    offset = (jnp.arange(N_POOL, dtype=jnp.int32) * REQS_DEV)[:, None]
    request = (local + offset).reshape(TOKENS)
    row_slot = adapter_pool_slot[request_adapter[:, 0][request]]
    query_base = jnp.dot(tokens, query_matrix, preferred_element_type=jnp.float32)
    key_all = jnp.dot(tokens, key_matrix, preferred_element_type=jnp.float32).astype(jnp.bfloat16)
    value_all = jnp.dot(tokens, value_matrix, preferred_element_type=jnp.float32).astype(jnp.bfloat16)

    def shrink_step(slot_number, running):
        weight_panel = lax.dynamic_index_in_dim(query_down_maps, slot_number, 0, keepdims=False)
        return jnp.where((row_slot == slot_number)[:, None], jnp.dot(tokens, weight_panel, preferred_element_type=jnp.float32), running)

    low_rank = lax.fori_loop(0, POOL_ADAPTERS, shrink_step, jnp.zeros((TOKENS, ADAPTER_RANK), jnp.float32)).astype(jnp.bfloat16)

    def expand_step(slot_number, running):
        weight_panel = lax.dynamic_index_in_dim(query_up_maps, slot_number, 0, keepdims=False)
        return jnp.where((row_slot == slot_number)[:, None], jnp.dot(low_rank, weight_panel, preferred_element_type=jnp.float32), running)

    delta = lax.fori_loop(0, POOL_ADAPTERS, expand_step, jnp.zeros((TOKENS, QUERY_WIDTH), jnp.float32)).astype(jnp.bfloat16)
    queries = (query_base + delta.astype(jnp.float32)).astype(jnp.bfloat16)
    blocks = (queries.reshape(N_POOL, TOK_DEV, QUERY_WIDTH), key_all.reshape(N_POOL, TOK_DEV, KW), value_all.reshape(N_POOL, TOK_DEV, KW), local)
    outputs = lax.map(lambda block: attend_block(block[0], block[1], block[2], block[3]), blocks)
    return outputs.reshape(TOKENS, QUERY_WIDTH)
```

```python
import functools

import jax
import jax.numpy as jnp
from jax import lax
from jax.experimental import pallas as pl
from jax.experimental.pallas import tpu as pltpu
from jax.sharding import PartitionSpec as P

HEAD_DIM = 128
LEN_MOST = 16


def request_local(lengths_row, tok_count):
    boundary = jnp.cumsum(lengths_row, dtype=jnp.int32)
    position = jnp.arange(tok_count, dtype=jnp.int32)
    return jnp.sum(
        (position[:, None] >= boundary[None, :]).astype(jnp.int32), axis=1, dtype=jnp.int32
    )


def attend_local(queries, key_vals, value_vals, request, head_dim):
    tok_count = queries.shape[0]
    kv_count = key_vals.shape[1] // head_dim
    group_size = queries.shape[1] // key_vals.shape[1]
    query_h = queries.reshape(tok_count, kv_count, group_size, head_dim)
    key_h = key_vals.reshape(tok_count, kv_count, head_dim)
    value_h = value_vals.reshape(tok_count, kv_count, head_dim)
    scores = jnp.einsum(
        "tkgd,skd->kgts", query_h, key_h, preferred_element_type=jnp.float32
    ) * head_dim ** (-0.5)
    position = jnp.arange(tok_count)
    allowed = (request[:, None] == request[None, :]) & (position[None, :] <= position[:, None])
    scores = jnp.where(allowed, scores, -1e30)
    top_score = jnp.max(scores, axis=-1, keepdims=True)
    exp_terms = jnp.exp(scores - top_score)
    softmax_w = (exp_terms / jnp.sum(exp_terms, axis=-1, keepdims=True)).astype(jnp.bfloat16)
    mixed = jnp.einsum("kgts,skd->tkgd", softmax_w, value_h, preferred_element_type=jnp.float32)
    return mixed.astype(jnp.bfloat16).reshape(tok_count, kv_count * group_size * head_dim)


def shards_gathered(
    tokens,
    query_matrix,
    key_matrix,
    value_matrix,
    query_down_maps,
    query_up_maps,
    request_lengths,
    request_adapter,
    adapter_pool_slot,
):
    tok_count = tokens.shape[0]
    feat_count = tokens.shape[1]
    req_count = request_lengths.shape[1]
    adapter_count = adapter_pool_slot.shape[0]
    capacity = max(2, req_count // adapter_count) * LEN_MOST
    request = request_local(request_lengths[0], tok_count)
    slot_table = jnp.sum(
        jnp.where(
            request_adapter[:, 0][:, None] == jnp.arange(adapter_count)[None, :],
            adapter_pool_slot[None, :],
            0,
        ),
        axis=1,
        dtype=jnp.int32,
    )
    row_slot = jnp.sum(
        jnp.where(request[:, None] == jnp.arange(req_count)[None, :], slot_table[None, :], 0),
        axis=1,
        dtype=jnp.int32,
    )
    slot_hit = (row_slot[:, None] == jnp.arange(adapter_count)[None, :]).astype(jnp.int32)
    earlier = jnp.cumsum(slot_hit, axis=0, dtype=jnp.int32) - slot_hit
    target = row_slot * capacity + jnp.sum(earlier * slot_hit, axis=1, dtype=jnp.int32)
    packed = jnp.zeros((adapter_count * capacity, feat_count), jnp.bfloat16).at[target].set(tokens)
    packed = packed.reshape(adapter_count, capacity, feat_count)
    tok_full = lax.all_gather(tokens, "tp", axis=1, tiled=True)
    pieces = (
        lax.all_gather(query_matrix, "pool", axis=0, tiled=True),
        lax.all_gather(key_matrix, "pool", axis=0, tiled=True),
        lax.all_gather(value_matrix, "pool", axis=0, tiled=True),
    )
    query_base, key_raw, value_raw = tuple(
        (
            jnp.dot(tok_full, weight_piece, preferred_element_type=jnp.float32)
            for weight_piece in pieces
        )
    )
    shrunk = jnp.einsum(
        "sjd,sdr->sjr",
        packed,
        lax.all_gather(query_down_maps, "pool", axis=0, tiled=True),
        preferred_element_type=jnp.float32,
    )
    low_rank = lax.psum(shrunk, "tp").astype(jnp.bfloat16)
    delta = jnp.einsum(
        "sjr,srk->sjk",
        low_rank,
        lax.all_gather(query_up_maps, "pool", axis=0, tiled=True),
        preferred_element_type=jnp.float32,
    ).astype(jnp.bfloat16)
    delta_tokens = delta.reshape(adapter_count * capacity, delta.shape[2])[target]
    queries = (query_base + delta_tokens.astype(jnp.float32)).astype(jnp.bfloat16)
    return attend_local(
        queries, key_raw.astype(jnp.bfloat16), value_raw.astype(jnp.bfloat16), request, HEAD_DIM
    )


UNIT = 128
A_UNITS = 6


def attend_kernel(group_size, q_ref, k_ref, v_ref, bias_ref, out_ref):
    blocks = q_ref.shape[0] // UNIT
    kv_count = k_ref.shape[1] // HEAD_DIM
    for kv in range(kv_count):
        kv_cols = slice(kv * HEAD_DIM, (kv + 1) * HEAD_DIM)
        heads = [slice((kv * group_size + i) * HEAD_DIM, (kv * group_size + i + 1) * HEAD_DIM) for i in range(group_size)]
        for b in range(blocks):
            rows = slice(b * UNIT, (b + 1) * UNIT)
            keys = slice(max(0, b - 1) * UNIT, (b + 1) * UNIT)
            bias = bias_ref[b] if b > 0 else bias_ref[b][:, UNIT:]
            query = jnp.concatenate([q_ref[rows, cols] for cols in heads], axis=0)
            scores = lax.dot_general(
                query, k_ref[keys, kv_cols], (((1,), (1,)), ((), ())), preferred_element_type=jnp.float32
            ) * HEAD_DIM ** (-0.5)
            scores = scores + jnp.concatenate([bias] * group_size, axis=0)
            exp_terms = jnp.exp(scores - jnp.max(scores, axis=-1, keepdims=True))
            weights = (exp_terms / jnp.sum(exp_terms, axis=-1, keepdims=True)).astype(jnp.bfloat16)
            mixed = jnp.dot(weights, v_ref[keys, kv_cols], preferred_element_type=jnp.float32).astype(jnp.bfloat16)
            for i, cols in enumerate(heads):
                out_ref[rows, cols] = mixed[i * UNIT : (i + 1) * UNIT]


def request_bias(request):
    blocks = request.shape[0] // UNIT
    padded = jnp.concatenate([jnp.full((UNIT,), -1, jnp.int32), request])
    keys = jnp.stack([padded[b * UNIT : (b + 2) * UNIT] for b in range(blocks)])
    row = jnp.arange(UNIT)[:, None]
    col = jnp.arange(2 * UNIT)[None, :]
    allowed = (request.reshape(blocks, UNIT, 1) == keys[:, None, :]) & (col <= row + UNIT)[None]
    return jnp.where(allowed, 0.0, -1e30).astype(jnp.float32)


def swap(x, axis, count, bit):
    return lax.ppermute(x, axis, [(i, i ^ bit) for i in range(count)])


def line_gather(x, axis, count):
    ups, downs, up, down = [], [], x, x
    for k in range(1, count):
        up = lax.ppermute(up, axis, [(i, i + 1) for i in range(k - 1, count - 1)])
        down = lax.ppermute(down, axis, [(i, i - 1) for i in range(1, count - k + 1)])
        ups.append(up)
        downs.append(down)
    return ups, downs


def ring_order(x, ups, downs, count):
    return [x] + [ups[k - 1] + downs[count - k - 1] for k in range(1, count)]


def shards_summed(
    pools,
    tokens,
    query_matrix,
    key_matrix,
    value_matrix,
    query_down_maps,
    query_up_maps,
    request_lengths,
    request_adapter,
    adapter_pool_slot,
):
    tok_count, feat_count = tokens.shape
    req_count = request_lengths.shape[1]
    adapter_count = adapter_pool_slot.shape[0]
    slots_own, _, rank = query_down_maps.shape
    group, pool, part = lax.axis_index("groups"), lax.axis_index("pool"), lax.axis_index("tp")
    f32, bf16 = jnp.float32, jnp.bfloat16
    dot = functools.partial(jnp.dot, preferred_element_type=f32)

    request = request_local(request_lengths[0], tok_count)
    slot_table = jnp.sum(
        jnp.where(
            request_adapter[:, 0][:, None] == jnp.arange(adapter_count)[None, :],
            adapter_pool_slot[None, :],
            0,
        ),
        axis=1,
        dtype=jnp.int32,
    )
    row_slot = jnp.sum(
        jnp.where(request[:, None] == jnp.arange(req_count)[None, :], slot_table[None, :], 0),
        axis=1,
        dtype=jnp.int32,
    )
    bias = request_bias(request)

    kv_count = key_matrix.shape[1] // HEAD_DIM
    per_kv = query_matrix.shape[1] // key_matrix.shape[1]
    units = []
    for kv in range(kv_count):
        units.append(key_matrix[:, kv * HEAD_DIM : (kv + 1) * HEAD_DIM])
        units.append(value_matrix[:, kv * HEAD_DIM : (kv + 1) * HEAD_DIM])
        for i in range(kv * per_kv, (kv + 1) * per_kv):
            units.append(query_matrix[:, i * HEAD_DIM : (i + 1) * HEAD_DIM])
    moved_w = jnp.concatenate(units[:A_UNITS], axis=1)
    kept_w = jnp.concatenate(units[A_UNITS:], axis=1)

    tok_x = swap(tokens, "tp", pools, 2)
    tok_parts = jnp.stack([tokens, swap(tokens, "tp", pools, 1), tok_x, swap(tok_x, "tp", pools, 1)])

    def features(block):
        return lax.dynamic_index_in_dim(tok_parts, block ^ part, 0, keepdims=False)

    half = moved_w.shape[0] // 2
    own_half = lax.dynamic_slice_in_dim(moved_w, group * half, half, 0)
    ups, downs = line_gather(own_half, "pool", pools)

    def other_half(x, first, last):
        pairs = [(g * pools + i, (1 - g) * pools + i) for g in range(2) for i in range(first, last)]
        return lax.ppermute(x, ("groups", "pool"), pairs)

    moved = dot(features(pool), moved_w)
    for k in range(1, pools):
        for arrived, block, first, last in (
            (ups[k - 1], (pool - k) % pools, k, pools),
            (downs[k - 1], (pool + k) % pools, 0, pools - k),
        ):
            feats = features(block)
            moved += dot(lax.dynamic_slice_in_dim(feats, group * half, half, 1), arrived)
            moved += dot(
                lax.dynamic_slice_in_dim(feats, (1 - group) * half, half, 1), other_half(arrived, first, last)
            )

    quarter = tok_count // pools

    def partial_of(bit):
        mine = lax.dynamic_slice_in_dim(features(pool ^ bit), part * quarter, quarter, 0)
        mine = lax.ppermute(mine, "pool", [(i, i ^ bit) for i in range(pools)])
        mine_x = swap(mine, "tp", pools, 2)
        stacked = jnp.stack([mine, swap(mine, "tp", pools, 1), mine_x, swap(mine_x, "tp", pools, 1)])
        rows = jnp.concatenate(
            [lax.dynamic_index_in_dim(stacked, part ^ i, 0, keepdims=False) for i in range(pools)], axis=0
        )
        return dot(rows, kept_w)

    far, mid, near = partial_of(3), partial_of(2), partial_of(1)
    up = lax.ppermute(far.astype(bf16), "pool", [(0, 1)])
    down = lax.ppermute(far.astype(bf16), "pool", [(3, 2)])
    up = lax.ppermute((up + mid).astype(bf16), "pool", [(0, 1), (1, 2)])
    down = lax.ppermute((down + mid).astype(bf16), "pool", [(3, 2), (2, 1)])
    up = lax.ppermute((up + jnp.where(pool == 1, far, near)).astype(bf16), "pool", [(0, 1), (1, 2), (2, 3)])
    down = lax.ppermute((down + jnp.where(pool == 2, far, near)).astype(bf16), "pool", [(3, 2), (2, 1), (1, 0)])
    kept = dot(features(pool), kept_w) + up + down

    down_maps = ring_order(query_down_maps, *line_gather(query_down_maps, "pool", pools), pools)
    up_maps = ring_order(query_up_maps, *line_gather(query_up_maps, "pool", pools), pools)
    shrunk = jnp.zeros((tok_count, rank), f32)
    for k in range(pools):
        for i in range(slots_own):
            here = row_slot == ((pool - k) % pools) * slots_own + i
            shrunk += jnp.where(here[:, None], dot(tokens, down_maps[k][i]), 0.0)
    shrunk += swap(shrunk, "tp", pools, 2)
    shrunk += swap(shrunk, "tp", pools, 1)
    low_rank = shrunk.astype(bf16)
    delta = jnp.zeros((tok_count, query_matrix.shape[1]), f32)
    for k in range(pools):
        for i in range(slots_own):
            here = row_slot == ((pool - k) % pools) * slots_own + i
            delta += dot(jnp.where(here[:, None], low_rank, 0), up_maps[k][i])
    delta = delta.astype(bf16).astype(f32)

    whole = jnp.concatenate([moved, kept], axis=1)
    span = (per_kv + 2) * HEAD_DIM
    keys = jnp.concatenate([whole[:, kv * span : kv * span + HEAD_DIM] for kv in range(kv_count)], axis=1)
    values = jnp.concatenate(
        [whole[:, kv * span + HEAD_DIM : kv * span + 2 * HEAD_DIM] for kv in range(kv_count)], axis=1
    )
    base = jnp.concatenate(
        [whole[:, kv * span + 2 * HEAD_DIM : (kv + 1) * span] for kv in range(kv_count)], axis=1
    )
    queries = (base + delta).astype(bf16)
    return pl.pallas_call(
        functools.partial(attend_kernel, per_kv),
        out_shape=jax.ShapeDtypeStruct(queries.shape, bf16),
        compiler_params=pltpu.CompilerParams(vmem_limit_bytes=32 * 2**20),
    )(queries, keys.astype(bf16), values.astype(bf16), bias)


def solution(mesh):
    placed = (
        P(("groups", "pool"), "tp"),
        P("pool", "tp"),
        P("pool", "tp"),
        P("pool", "tp"),
        P(("groups", "pool"), "tp", None),
        P(("groups", "pool"), None, "tp"),
        P(("groups", "pool"), None),
        P(("groups", "pool"), None),
        P(),
    )
    sizes = mesh.shape
    if sizes["groups"] == 2 and sizes["pool"] == 4 and sizes["tp"] == 4:
        shards = functools.partial(shards_summed, sizes["pool"])
    else:
        shards = shards_gathered
    return jax.shard_map(
        shards, mesh=mesh, in_specs=placed, out_specs=P(("groups", "pool"), "tp"), check_vma=False
    )
```

```python
import functools

import jax
import jax.numpy as jnp
from jax import lax
from jax.experimental import pallas as pl
from jax.experimental.pallas import tpu as pltpu
from jax.sharding import PartitionSpec as P

HEAD_DIM = 128
LEN_MOST = 16


def request_local(lengths_row, tok_count):
    boundary = jnp.cumsum(lengths_row, dtype=jnp.int32)
    position = jnp.arange(tok_count, dtype=jnp.int32)
    return jnp.sum(
        (position[:, None] >= boundary[None, :]).astype(jnp.int32), axis=1, dtype=jnp.int32
    )


def attend_local(queries, key_vals, value_vals, request, head_dim):
    tok_count = queries.shape[0]
    kv_count = key_vals.shape[1] // head_dim
    group_size = queries.shape[1] // key_vals.shape[1]
    query_h = queries.reshape(tok_count, kv_count, group_size, head_dim)
    key_h = key_vals.reshape(tok_count, kv_count, head_dim)
    value_h = value_vals.reshape(tok_count, kv_count, head_dim)
    scores = jnp.einsum(
        "tkgd,skd->kgts", query_h, key_h, preferred_element_type=jnp.float32
    ) * head_dim ** (-0.5)
    position = jnp.arange(tok_count)
    allowed = (request[:, None] == request[None, :]) & (position[None, :] <= position[:, None])
    scores = jnp.where(allowed, scores, -1e30)
    top_score = jnp.max(scores, axis=-1, keepdims=True)
    exp_terms = jnp.exp(scores - top_score)
    softmax_w = (exp_terms / jnp.sum(exp_terms, axis=-1, keepdims=True)).astype(jnp.bfloat16)
    mixed = jnp.einsum("kgts,skd->tkgd", softmax_w, value_h, preferred_element_type=jnp.float32)
    return mixed.astype(jnp.bfloat16).reshape(tok_count, kv_count * group_size * head_dim)


def shards_gathered(
    tokens,
    query_matrix,
    key_matrix,
    value_matrix,
    query_down_maps,
    query_up_maps,
    request_lengths,
    request_adapter,
    adapter_pool_slot,
):
    tok_count = tokens.shape[0]
    feat_count = tokens.shape[1]
    req_count = request_lengths.shape[1]
    adapter_count = adapter_pool_slot.shape[0]
    capacity = max(2, req_count // adapter_count) * LEN_MOST
    request = request_local(request_lengths[0], tok_count)
    slot_table = jnp.sum(
        jnp.where(
            request_adapter[:, 0][:, None] == jnp.arange(adapter_count)[None, :],
            adapter_pool_slot[None, :],
            0,
        ),
        axis=1,
        dtype=jnp.int32,
    )
    row_slot = jnp.sum(
        jnp.where(request[:, None] == jnp.arange(req_count)[None, :], slot_table[None, :], 0),
        axis=1,
        dtype=jnp.int32,
    )
    slot_hit = (row_slot[:, None] == jnp.arange(adapter_count)[None, :]).astype(jnp.int32)
    earlier = jnp.cumsum(slot_hit, axis=0, dtype=jnp.int32) - slot_hit
    target = row_slot * capacity + jnp.sum(earlier * slot_hit, axis=1, dtype=jnp.int32)
    packed = jnp.zeros((adapter_count * capacity, feat_count), jnp.bfloat16).at[target].set(tokens)
    packed = packed.reshape(adapter_count, capacity, feat_count)
    tok_full = lax.all_gather(tokens, "tp", axis=1, tiled=True)
    pieces = (
        lax.all_gather(query_matrix, "pool", axis=0, tiled=True),
        lax.all_gather(key_matrix, "pool", axis=0, tiled=True),
        lax.all_gather(value_matrix, "pool", axis=0, tiled=True),
    )
    query_base, key_raw, value_raw = tuple(
        (
            jnp.dot(tok_full, weight_piece, preferred_element_type=jnp.float32)
            for weight_piece in pieces
        )
    )
    shrunk = jnp.einsum(
        "sjd,sdr->sjr",
        packed,
        lax.all_gather(query_down_maps, "pool", axis=0, tiled=True),
        preferred_element_type=jnp.float32,
    )
    low_rank = lax.psum(shrunk, "tp").astype(jnp.bfloat16)
    delta = jnp.einsum(
        "sjr,srk->sjk",
        low_rank,
        lax.all_gather(query_up_maps, "pool", axis=0, tiled=True),
        preferred_element_type=jnp.float32,
    ).astype(jnp.bfloat16)
    delta_tokens = delta.reshape(adapter_count * capacity, delta.shape[2])[target]
    queries = (query_base + delta_tokens.astype(jnp.float32)).astype(jnp.bfloat16)
    return attend_local(
        queries, key_raw.astype(jnp.bfloat16), value_raw.astype(jnp.bfloat16), request, HEAD_DIM
    )


UNIT = 128


def attend_kernel(group_size, own_ref, near_ref, far_ref, delta_ref, bias_ref, *refs):
    out_ref, sum_ref = refs[-2:]
    wide = (own_ref[...] + near_ref[...].astype(jnp.float32)) + far_ref[...].astype(jnp.float32)
    sum_ref[:, : 2 * HEAD_DIM] = wide[:, : 2 * HEAD_DIM].astype(jnp.bfloat16)
    sum_ref[:, 2 * HEAD_DIM :] = (wide[:, 2 * HEAD_DIM :] + delta_ref[...].astype(jnp.float32)).astype(jnp.bfloat16)
    for b in range(own_ref.shape[0] // UNIT):
        rows = slice(b * UNIT, (b + 1) * UNIT)
        keys = slice(max(0, b - 1) * UNIT, (b + 1) * UNIT)
        bias = bias_ref[b] if b > 0 else bias_ref[b][:, UNIT:]
        query = jnp.concatenate(
            [sum_ref[rows, (2 + i) * HEAD_DIM : (3 + i) * HEAD_DIM] for i in range(group_size)], axis=0
        )
        scores = lax.dot_general(
            query, sum_ref[keys, :HEAD_DIM], (((1,), (1,)), ((), ())), preferred_element_type=jnp.float32
        ) * HEAD_DIM ** (-0.5)
        scores = scores + jnp.concatenate([bias] * group_size, axis=0)
        exp_terms = jnp.exp(scores - jnp.max(scores, axis=-1, keepdims=True))
        weights = (exp_terms / jnp.sum(exp_terms, axis=-1, keepdims=True)).astype(jnp.bfloat16)
        mixed = jnp.dot(
            weights, sum_ref[keys, HEAD_DIM : 2 * HEAD_DIM], preferred_element_type=jnp.float32
        ).astype(jnp.bfloat16)
        for i in range(group_size):
            out_ref[rows, i * HEAD_DIM : (i + 1) * HEAD_DIM] = mixed[i * UNIT : (i + 1) * UNIT]


def attend_head(kv, kv_count, own, near, far, delta, bias, earlier):
    rows, span = own.shape
    group_size = span // HEAD_DIM - 2
    wide = group_size * HEAD_DIM
    whole = [pl.BlockSpec(x.shape, lambda i, n=x.ndim: (0,) * n) for x in (own, near, far)]
    specs = whole + [pl.BlockSpec((rows, wide), lambda i: (0, kv)), pl.BlockSpec(bias.shape, lambda i: (0, 0, 0))]
    operands = [own, near, far, delta, bias]
    aliases = {}
    if earlier is not None:
        specs.append(pl.BlockSpec(memory_space=pl.ANY))
        operands.append(earlier)
        aliases = {5: 0}
    return pl.pallas_call(
        functools.partial(attend_kernel, group_size),
        grid=(1,),
        in_specs=specs,
        out_specs=pl.BlockSpec((rows, wide), lambda i: (0, kv)),
        out_shape=jax.ShapeDtypeStruct((rows, kv_count * wide), jnp.bfloat16),
        scratch_shapes=[pltpu.VMEM((rows, span), jnp.bfloat16)],
        input_output_aliases=aliases,
        compiler_params=pltpu.CompilerParams(vmem_limit_bytes=32 * 2**20),
        cost_estimate=pl.CostEstimate(flops=4 * rows * 256 * wide, bytes_accessed=12 * rows * span, transcendentals=rows * 256 * group_size),
    )(*operands)


def request_bias(request):
    blocks = request.shape[0] // UNIT
    padded = jnp.concatenate([jnp.full((UNIT,), -1, jnp.int32), request])
    keys = jnp.stack([padded[b * UNIT : (b + 2) * UNIT] for b in range(blocks)])
    row = jnp.arange(UNIT)[:, None]
    col = jnp.arange(2 * UNIT)[None, :]
    allowed = (request.reshape(blocks, UNIT, 1) == keys[:, None, :]) & (col <= row + UNIT)[None]
    return jnp.where(allowed, 0.0, -1e30).astype(jnp.float32)


PAIRED = (4, 4, 2)
FAR = [(0, 2), (3, 1)]
INNER = [(1, 2), (2, 1)]
OUTWARD = [(1, 0), (2, 3)]


def shards_paired(
    tokens,
    query_matrix,
    key_matrix,
    value_matrix,
    query_down_maps,
    query_up_maps,
    request_lengths,
    request_adapter,
    adapter_pool_slot,
):
    pools, parts, groups = PAIRED
    tok_count, feat_count = tokens.shape
    req_count = request_lengths.shape[1]
    adapter_count = adapter_pool_slot.shape[0]
    slots_own, _, rank = query_down_maps.shape
    group, pool, part = lax.axis_index("groups"), lax.axis_index("pool"), lax.axis_index("tp")
    f32, bf16 = jnp.float32, jnp.bfloat16
    dot = functools.partial(jnp.dot, preferred_element_type=f32)
    here = part // 2 == pool // 2
    first_core = pool % 2 == part % 2

    def permute(x, axes, pairs):
        return lax.ppermute(x, axes, pairs)

    def chip_swap(x, inner_only):
        chosen = (1, 2) if inner_only else range(pools)
        return permute(x, ("pool", "tp"), [(p * parts + t, p * parts + (t ^ 2)) for p in chosen for t in range(parts)])

    def core_swap(x, inner_only):
        chosen = (1, 2) if inner_only else range(pools)
        return permute(x, ("pool", "tp"), [(p * parts + t, p * parts + (t ^ 1)) for p in chosen for t in range(parts)])

    half_rows = tok_count // 2
    top = chip_swap(tokens[:half_rows], False)
    leaving = jnp.where(here, top, tokens[half_rows:])

    kv_count = key_matrix.shape[1] // HEAD_DIM
    wide = query_matrix.shape[1] // kv_count
    half = feat_count // 2
    weights, theirs = [], []
    for kv in range(kv_count):
        cols = slice(kv * HEAD_DIM, (kv + 1) * HEAD_DIM)
        both = jnp.concatenate(
            [key_matrix[:, cols], value_matrix[:, cols], query_matrix[:, kv * wide : (kv + 1) * wide]], axis=1
        )
        weights.append(both)
        theirs.append(
            permute(
                lax.dynamic_slice_in_dim(both, group * half, half, 0), "pool", [(i, i ^ 1) for i in range(pools)]
            )
        )

    down_own = jnp.concatenate([query_down_maps[i] for i in range(slots_own)], axis=1)
    up_own = query_up_maps.reshape(slots_own * rank, -1)
    packed = jnp.concatenate([down_own, up_own.reshape(-1, slots_own * rank)], axis=0)
    pair_maps = jnp.stack([packed, permute(packed, "pool", [(i, i ^ 1) for i in range(pools)])])

    far = permute(leaving, "pool", FAR)
    near = permute(leaving, "pool", INNER)

    bottom = permute(
        tokens[half_rows:],
        ("pool", "tp"),
        [(p * parts + t, p * parts + (t ^ 2)) for p in range(pools) for t in range(parts) if t // 2 == p // 2],
    )
    mine = jnp.where(here, tokens, jnp.concatenate([top, bottom], axis=0))

    crossed = permute(pair_maps, "pool", INNER)

    def paired_features(block):
        other = core_swap(block[0], block[1])
        return jnp.where(first_core, block[0], other), jnp.where(first_core, other, block[0])

    def whole_rows(arrived):
        swapped = chip_swap(arrived, True)
        return jnp.concatenate([jnp.where(here, swapped, arrived), jnp.where(here, arrived, swapped)], axis=0)

    far_feats = paired_features((whole_rows(far), True))
    near_feats = paired_features((whole_rows(near), True))
    own_feats = paired_features((mine, False))

    other_theirs = [
        permute(x, ("groups", "pool"), [(g * pools + p, (1 - g) * pools + p) for g in range(groups) for p in range(pools)])
        for x in theirs
    ]

    def partial_sum(feats, kv):
        partner = feats[1]
        return (
            dot(feats[0], weights[kv])
            + dot(lax.dynamic_slice_in_dim(partner, group * half, half, 1), theirs[kv])
            + dot(lax.dynamic_slice_in_dim(partner, (1 - group) * half, half, 1), other_theirs[kv])
        )

    arrived_far = [permute(partial_sum(far_feats, kv).astype(bf16), "pool", INNER) for kv in range(kv_count)]
    outward = permute(crossed, "pool", OUTWARD)
    arrived_near = [permute(partial_sum(near_feats, kv).astype(bf16), "pool", INNER) for kv in range(kv_count)]
    forwarded = [permute(x, "pool", OUTWARD) for x in arrived_far]
    own = [partial_sum(own_feats, kv) for kv in range(kv_count)]

    request = request_local(request_lengths[0], tok_count)
    slot_table = jnp.sum(
        jnp.where(
            request_adapter[:, 0][:, None] == jnp.arange(adapter_count)[None, :],
            adapter_pool_slot[None, :],
            0,
        ),
        axis=1,
        dtype=jnp.int32,
    )
    row_slot = jnp.sum(
        jnp.where(request[:, None] == jnp.arange(req_count)[None, :], slot_table[None, :], 0),
        axis=1,
        dtype=jnp.int32,
    )
    bias = request_bias(request)
    maps = jnp.concatenate([pair_maps, crossed + outward], axis=0)
    inner = 2 - pool // 2
    holders = (pool, pool ^ 1, inner, inner ^ 1)
    chosen = [(row_slot == holder * slots_own + i)[:, None] for holder in holders for i in range(slots_own)]
    shrunk = jnp.zeros((tok_count, rank), f32)
    for k in range(pools):
        product = dot(tokens, maps[k, :feat_count])
        for i in range(slots_own):
            shrunk += jnp.where(chosen[k * slots_own + i], product[:, i * rank : (i + 1) * rank], 0.0)
    shrunk += core_swap(shrunk, False)
    shrunk += chip_swap(shrunk, False)
    low_rank = shrunk.astype(bf16)
    spread = jnp.concatenate([jnp.where(hit, low_rank, 0) for hit in chosen], axis=1)
    delta = dot(spread, maps[:, feat_count:].reshape(pools * slots_own * rank, -1)).astype(bf16)

    mixed = None
    for kv in range(kv_count):
        mixed = attend_head(kv, kv_count, own[kv], arrived_near[kv], forwarded[kv], delta, bias, mixed)
    return mixed


def solution(mesh):
    placed = (
        P(("groups", "pool"), "tp"),
        P("pool", "tp"),
        P("pool", "tp"),
        P("pool", "tp"),
        P(("groups", "pool"), "tp", None),
        P(("groups", "pool"), None, "tp"),
        P(("groups", "pool"), None),
        P(("groups", "pool"), None),
        P(),
    )
    sizes = mesh.shape
    if (sizes["pool"], sizes["tp"], sizes["groups"]) == PAIRED:
        shards = shards_paired
    else:
        shards = shards_gathered
    return jax.shard_map(
        shards, mesh=mesh, in_specs=placed, out_specs=P(("groups", "pool"), "tp"), check_vma=False
    )
```

```python
import functools

import jax
import jax.numpy as jnp
from jax import lax
from jax.experimental import pallas as pl
from jax.experimental.pallas import tpu as pltpu
from jax.sharding import PartitionSpec as P

HEAD_DIM = 128
LEN_MOST = 16


def request_local(lengths_row, tok_count):
    boundary = jnp.cumsum(lengths_row, dtype=jnp.int32)
    position = jnp.arange(tok_count, dtype=jnp.int32)
    return jnp.sum(
        (position[:, None] >= boundary[None, :]).astype(jnp.int32), axis=1, dtype=jnp.int32
    )


def attend_local(queries, key_vals, value_vals, request, head_dim):
    tok_count = queries.shape[0]
    kv_count = key_vals.shape[1] // head_dim
    group_size = queries.shape[1] // key_vals.shape[1]
    query_h = queries.reshape(tok_count, kv_count, group_size, head_dim)
    key_h = key_vals.reshape(tok_count, kv_count, head_dim)
    value_h = value_vals.reshape(tok_count, kv_count, head_dim)
    scores = jnp.einsum(
        "tkgd,skd->kgts", query_h, key_h, preferred_element_type=jnp.float32
    ) * head_dim ** (-0.5)
    position = jnp.arange(tok_count)
    allowed = (request[:, None] == request[None, :]) & (position[None, :] <= position[:, None])
    scores = jnp.where(allowed, scores, -1e30)
    top_score = jnp.max(scores, axis=-1, keepdims=True)
    exp_terms = jnp.exp(scores - top_score)
    softmax_w = (exp_terms / jnp.sum(exp_terms, axis=-1, keepdims=True)).astype(jnp.bfloat16)
    mixed = jnp.einsum("kgts,skd->tkgd", softmax_w, value_h, preferred_element_type=jnp.float32)
    return mixed.astype(jnp.bfloat16).reshape(tok_count, kv_count * group_size * head_dim)


def shards_gathered(
    tokens,
    query_matrix,
    key_matrix,
    value_matrix,
    query_down_maps,
    query_up_maps,
    request_lengths,
    request_adapter,
    adapter_pool_slot,
):
    tok_count = tokens.shape[0]
    feat_count = tokens.shape[1]
    req_count = request_lengths.shape[1]
    adapter_count = adapter_pool_slot.shape[0]
    capacity = max(2, req_count // adapter_count) * LEN_MOST
    request = request_local(request_lengths[0], tok_count)
    slot_table = jnp.sum(
        jnp.where(
            request_adapter[:, 0][:, None] == jnp.arange(adapter_count)[None, :],
            adapter_pool_slot[None, :],
            0,
        ),
        axis=1,
        dtype=jnp.int32,
    )
    row_slot = jnp.sum(
        jnp.where(request[:, None] == jnp.arange(req_count)[None, :], slot_table[None, :], 0),
        axis=1,
        dtype=jnp.int32,
    )
    slot_hit = (row_slot[:, None] == jnp.arange(adapter_count)[None, :]).astype(jnp.int32)
    earlier = jnp.cumsum(slot_hit, axis=0, dtype=jnp.int32) - slot_hit
    target = row_slot * capacity + jnp.sum(earlier * slot_hit, axis=1, dtype=jnp.int32)
    packed = jnp.zeros((adapter_count * capacity, feat_count), jnp.bfloat16).at[target].set(tokens)
    packed = packed.reshape(adapter_count, capacity, feat_count)
    tok_full = lax.all_gather(tokens, "tp", axis=1, tiled=True)
    pieces = (
        lax.all_gather(query_matrix, "pool", axis=0, tiled=True),
        lax.all_gather(key_matrix, "pool", axis=0, tiled=True),
        lax.all_gather(value_matrix, "pool", axis=0, tiled=True),
    )
    query_base, key_raw, value_raw = tuple(
        (
            jnp.dot(tok_full, weight_piece, preferred_element_type=jnp.float32)
            for weight_piece in pieces
        )
    )
    shrunk = jnp.einsum(
        "sjd,sdr->sjr",
        packed,
        lax.all_gather(query_down_maps, "pool", axis=0, tiled=True),
        preferred_element_type=jnp.float32,
    )
    low_rank = lax.psum(shrunk, "tp").astype(jnp.bfloat16)
    delta = jnp.einsum(
        "sjr,srk->sjk",
        low_rank,
        lax.all_gather(query_up_maps, "pool", axis=0, tiled=True),
        preferred_element_type=jnp.float32,
    ).astype(jnp.bfloat16)
    delta_tokens = delta.reshape(adapter_count * capacity, delta.shape[2])[target]
    queries = (query_base + delta_tokens.astype(jnp.float32)).astype(jnp.bfloat16)
    return attend_local(
        queries, key_raw.astype(jnp.bfloat16), value_raw.astype(jnp.bfloat16), request, HEAD_DIM
    )


UNIT = 128


def attend_kernel(group_size, own_ref, near_ref, far_ref, delta_ref, bias_ref, *refs):
    out_ref, sum_ref = refs[-2:]
    wide = (own_ref[...] + near_ref[...].astype(jnp.float32)) + far_ref[...].astype(jnp.float32)
    sum_ref[:, : 2 * HEAD_DIM] = wide[:, : 2 * HEAD_DIM].astype(jnp.bfloat16)
    sum_ref[:, 2 * HEAD_DIM :] = (wide[:, 2 * HEAD_DIM :] + delta_ref[...].astype(jnp.float32)).astype(jnp.bfloat16)
    for b in range(own_ref.shape[0] // UNIT):
        rows = slice(b * UNIT, (b + 1) * UNIT)
        keys = slice(max(0, b - 1) * UNIT, (b + 1) * UNIT)
        bias = bias_ref[b] if b > 0 else bias_ref[b][:, UNIT:]
        query = jnp.concatenate(
            [sum_ref[rows, (2 + i) * HEAD_DIM : (3 + i) * HEAD_DIM] for i in range(group_size)], axis=0
        )
        scores = lax.dot_general(
            query, sum_ref[keys, :HEAD_DIM], (((1,), (1,)), ((), ())), preferred_element_type=jnp.float32
        ) * HEAD_DIM ** (-0.5)
        scores = scores + jnp.concatenate([bias] * group_size, axis=0)
        exp_terms = jnp.exp(scores - jnp.max(scores, axis=-1, keepdims=True))
        weights = (exp_terms / jnp.sum(exp_terms, axis=-1, keepdims=True)).astype(jnp.bfloat16)
        mixed = jnp.dot(
            weights, sum_ref[keys, HEAD_DIM : 2 * HEAD_DIM], preferred_element_type=jnp.float32
        ).astype(jnp.bfloat16)
        for i in range(group_size):
            out_ref[rows, i * HEAD_DIM : (i + 1) * HEAD_DIM] = mixed[i * UNIT : (i + 1) * UNIT]


def attend_head(kv, kv_count, own, near, far, delta, bias, earlier):
    rows, span = own.shape
    group_size = span // HEAD_DIM - 2
    wide = group_size * HEAD_DIM
    whole = [pl.BlockSpec(x.shape, lambda i, n=x.ndim: (0,) * n) for x in (own, near, far)]
    specs = whole + [pl.BlockSpec((rows, wide), lambda i: (0, kv)), pl.BlockSpec(bias.shape, lambda i: (0, 0, 0))]
    operands = [own, near, far, delta, bias]
    aliases = {}
    if earlier is not None:
        specs.append(pl.BlockSpec(memory_space=pl.ANY))
        operands.append(earlier)
        aliases = {5: 0}
    return pl.pallas_call(
        functools.partial(attend_kernel, group_size),
        grid=(1,),
        in_specs=specs,
        out_specs=pl.BlockSpec((rows, wide), lambda i: (0, kv)),
        out_shape=jax.ShapeDtypeStruct((rows, kv_count * wide), jnp.bfloat16),
        scratch_shapes=[pltpu.VMEM((rows, span), jnp.bfloat16)],
        input_output_aliases=aliases,
        compiler_params=pltpu.CompilerParams(vmem_limit_bytes=32 * 2**20),
        cost_estimate=pl.CostEstimate(flops=4 * rows * 256 * wide, bytes_accessed=12 * rows * span, transcendentals=rows * 256 * group_size),
    )(*operands)


def request_bias(request):
    blocks = request.shape[0] // UNIT
    padded = jnp.concatenate([jnp.full((UNIT,), -1, jnp.int32), request])
    keys = jnp.stack([padded[b * UNIT : (b + 2) * UNIT] for b in range(blocks)])
    row = jnp.arange(UNIT)[:, None]
    col = jnp.arange(2 * UNIT)[None, :]
    allowed = (request.reshape(blocks, UNIT, 1) == keys[:, None, :]) & (col <= row + UNIT)[None]
    return jnp.where(allowed, 0.0, -1e30).astype(jnp.float32)


PAIRED = (4, 4, 2)
FAR = [(0, 2), (3, 1)]
INNER = [(1, 2), (2, 1)]
OUTWARD = [(1, 0), (2, 3)]


def shards_paired(
    tokens,
    query_matrix,
    key_matrix,
    value_matrix,
    query_down_maps,
    query_up_maps,
    request_lengths,
    request_adapter,
    adapter_pool_slot,
):
    pools, parts, groups = PAIRED
    tok_count, feat_count = tokens.shape
    req_count = request_lengths.shape[1]
    adapter_count = adapter_pool_slot.shape[0]
    slots_own, _, rank = query_down_maps.shape
    group, pool, part = lax.axis_index("groups"), lax.axis_index("pool"), lax.axis_index("tp")
    f32, bf16 = jnp.float32, jnp.bfloat16
    dot = functools.partial(jnp.dot, preferred_element_type=f32)
    here = part // 2 == pool // 2
    first_core = pool % 2 == part % 2

    def permute(name, x, axes, pairs):
        with jax.named_scope(name):
            return lax.ppermute(x, axes, pairs)

    def chip_swap(name, x, inner_only):
        chosen = (1, 2) if inner_only else range(pools)
        pairs = [(p * parts + t, p * parts + (t ^ 2)) for p in chosen for t in range(parts)]
        return permute(name, x, ("pool", "tp"), pairs)

    def core_swap(name, x, inner_only):
        chosen = (1, 2) if inner_only else range(pools)
        pairs = [(p * parts + t, p * parts + (t ^ 1)) for p in chosen for t in range(parts)]
        return permute(name, x, ("pool", "tp"), pairs)

    def after(x, *done):
        return lax.optimization_barrier((x,) + done)[0]

    half_rows = tok_count // 2
    top = chip_swap("tokens_top", tokens[:half_rows], False)

    kv_count = key_matrix.shape[1] // HEAD_DIM
    wide = query_matrix.shape[1] // kv_count
    half = feat_count // 2
    in_pairs = [(i, i ^ 1) for i in range(pools)]

    def columns(kv, first, count):
        cut = [
            lax.dynamic_slice(x, (first, kv * size), (count, size))
            for x, size in ((key_matrix, HEAD_DIM), (value_matrix, HEAD_DIM), (query_matrix, wide))
        ]
        return jnp.concatenate(cut, axis=1)

    theirs = [permute("weights_0", columns(0, group * half, half), "pool", in_pairs)]

    leaving = jnp.where(here, top, tokens[half_rows:])
    far = permute("tokens_far", leaving, "pool", FAR)
    near = permute("tokens_near", leaving, "pool", INNER)

    down_own = jnp.concatenate([query_down_maps[i] for i in range(slots_own)], axis=1)
    up_own = query_up_maps.reshape(slots_own * rank, -1)
    packed = jnp.concatenate([down_own, up_own.reshape(-1, slots_own * rank)], axis=0)
    pair_maps = jnp.stack([packed, permute("maps_pair", after(packed, theirs[0]), "pool", in_pairs)])
    for kv in range(1, kv_count):
        theirs.append(permute(f"weights_{kv}", columns(kv, after(group, pair_maps) * half, half), "pool", in_pairs))
    crossed = permute("maps_crossed", pair_maps, "pool", INNER)
    weights = [columns(kv, 0, feat_count) for kv in range(kv_count)]

    bottom = permute(
        "tokens_bottom",
        after(tokens, top)[half_rows:],
        ("pool", "tp"),
        [(p * parts + t, p * parts + (t ^ 2)) for p in range(pools) for t in range(parts) if t // 2 == p // 2],
    )
    mine = jnp.where(here, tokens, jnp.concatenate([top, bottom], axis=0))

    def paired_features(name, block, inner_only):
        other = core_swap(name + "_cores", block, inner_only)
        return jnp.where(first_core, block, other), jnp.where(first_core, other, block)

    def whole_rows(name, arrived):
        swapped = chip_swap(name + "_chips", arrived, True)
        return jnp.concatenate([jnp.where(here, swapped, arrived), jnp.where(here, arrived, swapped)], axis=0)

    far_feats = paired_features("far", whole_rows("far", far), True)
    near_feats = paired_features("near", whole_rows("near", near), True)
    own_feats = paired_features("own", mine, False)

    other_theirs = [
        permute(
            f"weights_{kv}_replicas",
            x,
            ("groups", "pool"),
            [(g * pools + p, (1 - g) * pools + p) for g in range(groups) for p in range(pools)],
        )
        for kv, x in enumerate(theirs)
    ]

    def partial_sum(feats, kv):
        partner = feats[1]
        return (
            dot(feats[0], weights[kv])
            + dot(lax.dynamic_slice_in_dim(partner, group * half, half, 1), theirs[kv])
            + dot(lax.dynamic_slice_in_dim(partner, (1 - group) * half, half, 1), other_theirs[kv])
        )

    arrived_far, arrived_near, forwarded = [], [], []
    for kv in range(kv_count):
        arrived_far.append(permute(f"sums_far_{kv}", partial_sum(far_feats, kv).astype(bf16), "pool", INNER))
        arrived_near.append(permute(f"sums_near_{kv}", partial_sum(near_feats, kv).astype(bf16), "pool", INNER))
        forwarded.append(permute(f"sums_out_{kv}", arrived_far[kv], "pool", OUTWARD))
    outward = permute("maps_out", crossed, "pool", OUTWARD)
    own = [partial_sum(own_feats, kv) for kv in range(kv_count)]

    request = request_local(request_lengths[0], tok_count)
    slot_table = jnp.sum(
        jnp.where(
            request_adapter[:, 0][:, None] == jnp.arange(adapter_count)[None, :],
            adapter_pool_slot[None, :],
            0,
        ),
        axis=1,
        dtype=jnp.int32,
    )
    row_slot = jnp.sum(
        jnp.where(request[:, None] == jnp.arange(req_count)[None, :], slot_table[None, :], 0),
        axis=1,
        dtype=jnp.int32,
    )
    bias = request_bias(request)
    maps = jnp.concatenate([pair_maps, crossed + outward], axis=0)
    inner = 2 - pool // 2
    holders = (pool, pool ^ 1, inner, inner ^ 1)
    chosen = [(row_slot == holder * slots_own + i)[:, None] for holder in holders for i in range(slots_own)]
    shrunk = jnp.zeros((tok_count, rank), f32)
    for k in range(pools):
        product = dot(tokens, maps[k, :feat_count])
        for i in range(slots_own):
            shrunk += jnp.where(chosen[k * slots_own + i], product[:, i * rank : (i + 1) * rank], 0.0)
    shrunk += core_swap("low_rank_cores", shrunk, False)
    shrunk += chip_swap("low_rank_chips", shrunk, False)
    low_rank = shrunk.astype(bf16)
    spread = jnp.concatenate([jnp.where(hit, low_rank, 0) for hit in chosen], axis=1)
    delta = dot(spread, maps[:, feat_count:].reshape(pools * slots_own * rank, -1)).astype(bf16)

    mixed = None
    for kv in range(kv_count):
        mixed = attend_head(kv, kv_count, own[kv], arrived_near[kv], forwarded[kv], delta, bias, mixed)
    return mixed


def solution(mesh):
    placed = (
        P(("groups", "pool"), "tp"),
        P("pool", "tp"),
        P("pool", "tp"),
        P("pool", "tp"),
        P(("groups", "pool"), "tp", None),
        P(("groups", "pool"), None, "tp"),
        P(("groups", "pool"), None),
        P(("groups", "pool"), None),
        P(),
    )
    sizes = mesh.shape
    if (sizes["pool"], sizes["tp"], sizes["groups"]) == PAIRED:
        shards = shards_paired
    else:
        shards = shards_gathered
    return jax.shard_map(
        shards, mesh=mesh, in_specs=placed, out_specs=P(("groups", "pool"), "tp"), check_vma=False
    )
```

```python
import functools

import jax
import jax.numpy as jnp
from jax import lax
from jax.experimental import pallas as pl
from jax.experimental.pallas import tpu as pltpu
from jax.sharding import PartitionSpec as P

HEAD_DIM = 128
LEN_MOST = 16


def request_local(lengths_row, tok_count):
    boundary = jnp.cumsum(lengths_row, dtype=jnp.int32)
    position = jnp.arange(tok_count, dtype=jnp.int32)
    return jnp.sum(
        (position[:, None] >= boundary[None, :]).astype(jnp.int32), axis=1, dtype=jnp.int32
    )


def attend_local(queries, key_vals, value_vals, request, head_dim):
    tok_count = queries.shape[0]
    kv_count = key_vals.shape[1] // head_dim
    group_size = queries.shape[1] // key_vals.shape[1]
    query_h = queries.reshape(tok_count, kv_count, group_size, head_dim)
    key_h = key_vals.reshape(tok_count, kv_count, head_dim)
    value_h = value_vals.reshape(tok_count, kv_count, head_dim)
    scores = jnp.einsum(
        "tkgd,skd->kgts", query_h, key_h, preferred_element_type=jnp.float32
    ) * head_dim ** (-0.5)
    position = jnp.arange(tok_count)
    allowed = (request[:, None] == request[None, :]) & (position[None, :] <= position[:, None])
    scores = jnp.where(allowed, scores, -1e30)
    top_score = jnp.max(scores, axis=-1, keepdims=True)
    exp_terms = jnp.exp(scores - top_score)
    softmax_w = (exp_terms / jnp.sum(exp_terms, axis=-1, keepdims=True)).astype(jnp.bfloat16)
    mixed = jnp.einsum("kgts,skd->tkgd", softmax_w, value_h, preferred_element_type=jnp.float32)
    return mixed.astype(jnp.bfloat16).reshape(tok_count, kv_count * group_size * head_dim)


def shards_gathered(
    tokens,
    query_matrix,
    key_matrix,
    value_matrix,
    query_down_maps,
    query_up_maps,
    request_lengths,
    request_adapter,
    adapter_pool_slot,
):
    tok_count = tokens.shape[0]
    feat_count = tokens.shape[1]
    req_count = request_lengths.shape[1]
    adapter_count = adapter_pool_slot.shape[0]
    capacity = max(2, req_count // adapter_count) * LEN_MOST
    request = request_local(request_lengths[0], tok_count)
    slot_table = jnp.sum(
        jnp.where(
            request_adapter[:, 0][:, None] == jnp.arange(adapter_count)[None, :],
            adapter_pool_slot[None, :],
            0,
        ),
        axis=1,
        dtype=jnp.int32,
    )
    row_slot = jnp.sum(
        jnp.where(request[:, None] == jnp.arange(req_count)[None, :], slot_table[None, :], 0),
        axis=1,
        dtype=jnp.int32,
    )
    slot_hit = (row_slot[:, None] == jnp.arange(adapter_count)[None, :]).astype(jnp.int32)
    earlier = jnp.cumsum(slot_hit, axis=0, dtype=jnp.int32) - slot_hit
    target = row_slot * capacity + jnp.sum(earlier * slot_hit, axis=1, dtype=jnp.int32)
    packed = jnp.zeros((adapter_count * capacity, feat_count), jnp.bfloat16).at[target].set(tokens)
    packed = packed.reshape(adapter_count, capacity, feat_count)
    tok_full = lax.all_gather(tokens, "tp", axis=1, tiled=True)
    pieces = (
        lax.all_gather(query_matrix, "pool", axis=0, tiled=True),
        lax.all_gather(key_matrix, "pool", axis=0, tiled=True),
        lax.all_gather(value_matrix, "pool", axis=0, tiled=True),
    )
    query_base, key_raw, value_raw = tuple(
        (
            jnp.dot(tok_full, weight_piece, preferred_element_type=jnp.float32)
            for weight_piece in pieces
        )
    )
    shrunk = jnp.einsum(
        "sjd,sdr->sjr",
        packed,
        lax.all_gather(query_down_maps, "pool", axis=0, tiled=True),
        preferred_element_type=jnp.float32,
    )
    low_rank = lax.psum(shrunk, "tp").astype(jnp.bfloat16)
    delta = jnp.einsum(
        "sjr,srk->sjk",
        low_rank,
        lax.all_gather(query_up_maps, "pool", axis=0, tiled=True),
        preferred_element_type=jnp.float32,
    ).astype(jnp.bfloat16)
    delta_tokens = delta.reshape(adapter_count * capacity, delta.shape[2])[target]
    queries = (query_base + delta_tokens.astype(jnp.float32)).astype(jnp.bfloat16)
    return attend_local(
        queries, key_raw.astype(jnp.bfloat16), value_raw.astype(jnp.bfloat16), request, HEAD_DIM
    )


UNIT = 128


def attend_kernel(group_size, place_ref, own_ref, near_ref, far_ref, delta_ref, bias_ref, *refs):
    out_ref, sum_ref = refs[-2:]
    wide = own_ref[...] + jnp.where(place_ref[3] == 1, near_ref[...], far_ref[...]).astype(jnp.float32)
    sum_ref[:, : 2 * HEAD_DIM] = wide[:, : 2 * HEAD_DIM].astype(jnp.bfloat16)
    sum_ref[:, 2 * HEAD_DIM :] = (wide[:, 2 * HEAD_DIM :] + delta_ref[...].astype(jnp.float32)).astype(jnp.bfloat16)
    for b in range(own_ref.shape[0] // UNIT):
        rows = slice(b * UNIT, (b + 1) * UNIT)
        keys = slice(max(0, b - 1) * UNIT, (b + 1) * UNIT)
        bias = bias_ref[b] if b > 0 else bias_ref[b][:, UNIT:]
        query = jnp.concatenate(
            [sum_ref[rows, (2 + i) * HEAD_DIM : (3 + i) * HEAD_DIM] for i in range(group_size)], axis=0
        )
        scores = lax.dot_general(
            query, sum_ref[keys, :HEAD_DIM], (((1,), (1,)), ((), ())), preferred_element_type=jnp.float32
        ) * HEAD_DIM ** (-0.5)
        scores = scores + jnp.concatenate([bias] * group_size, axis=0)
        exp_terms = jnp.exp(scores - jnp.max(scores, axis=-1, keepdims=True))
        weights = (exp_terms / jnp.sum(exp_terms, axis=-1, keepdims=True)).astype(jnp.bfloat16)
        mixed = jnp.dot(
            weights, sum_ref[keys, HEAD_DIM : 2 * HEAD_DIM], preferred_element_type=jnp.float32
        ).astype(jnp.bfloat16)
        for i in range(group_size):
            out_ref[rows, i * HEAD_DIM : (i + 1) * HEAD_DIM] = mixed[i * UNIT : (i + 1) * UNIT]


def attend_head(kv, kv_count, place, own, near, far, delta, bias, earlier):
    rows, span = own.shape
    group_size = span // HEAD_DIM - 2
    wide = group_size * HEAD_DIM
    whole = [pl.BlockSpec((rows, span), lambda i, b=x.shape[0] // rows - 1: (b, 0)) for x in (own, near, far)]
    specs = [pl.BlockSpec(memory_space=pltpu.SMEM)] + whole + [pl.BlockSpec((rows, wide), lambda i: (0, kv)), pl.BlockSpec(bias.shape, lambda i: (0, 0, 0))]
    operands = [place, own, near, far, delta, bias]
    aliases = {}
    if earlier is not None:
        specs.append(pl.BlockSpec(memory_space=pl.ANY))
        operands.append(earlier)
        aliases = {6: 0}
    return pl.pallas_call(
        functools.partial(attend_kernel, group_size),
        grid=(1,),
        in_specs=specs,
        out_specs=pl.BlockSpec((rows, wide), lambda i: (0, kv)),
        out_shape=jax.ShapeDtypeStruct((rows, kv_count * wide), jnp.bfloat16),
        scratch_shapes=[pltpu.VMEM((rows, span), jnp.bfloat16)],
        input_output_aliases=aliases,
        compiler_params=pltpu.CompilerParams(vmem_limit_bytes=32 * 2**20),
        cost_estimate=pl.CostEstimate(flops=0, bytes_accessed=0, transcendentals=0),
    )(*operands)


def request_bias(request):
    blocks = request.shape[0] // UNIT
    padded = jnp.concatenate([jnp.full((UNIT,), -1, jnp.int32), request])
    keys = jnp.stack([padded[b * UNIT : (b + 2) * UNIT] for b in range(blocks)])
    row = jnp.arange(UNIT)[:, None]
    col = jnp.arange(2 * UNIT)[None, :]
    allowed = (request.reshape(blocks, UNIT, 1) == keys[:, None, :]) & (col <= row + UNIT)[None]
    return jnp.where(allowed, 0.0, -1e30).astype(jnp.float32)


def cut_kernel(kv, place_ref, tok_ref, key_ref, value_ref, query_ref, *refs):
    send, sems = refs[-2:]
    half, wide = send.shape[0], send.shape[1] - 2 * HEAD_DIM
    rows = pl.ds(pl.multiple_of(place_ref[2] * half, 64), half)
    pairs = []
    for i, token_ref in enumerate(refs[:-2]):
        pairs.append((tok_ref.at[pl.ds(i * token_ref.shape[0], token_ref.shape[0])], token_ref))
    small = pl.ds(kv * HEAD_DIM, HEAD_DIM)
    pairs.append((key_ref.at[rows, small], send.at[:, pl.ds(0, HEAD_DIM)]))
    pairs.append((value_ref.at[rows, small], send.at[:, pl.ds(HEAD_DIM, HEAD_DIM)]))
    pairs.append((query_ref.at[rows, pl.ds(kv * wide, wide)], send.at[:, pl.ds(2 * HEAD_DIM, wide)]))
    copies = [pltpu.make_async_copy(*pair, sems.at[i]) for i, pair in enumerate(pairs)]
    for copy in copies:
        copy.start()
    for copy in copies:
        copy.wait()


def cut(kv, place, tokens, key_matrix, value_matrix, query_matrix):
    rows, feats = tokens.shape
    kv_count = key_matrix.shape[1] // HEAD_DIM
    halves = [jax.ShapeDtypeStruct((rows // 2, feats), tokens.dtype)] * (2 if kv == 0 else 0)
    span = 2 * HEAD_DIM + query_matrix.shape[1] // kv_count
    send = jax.ShapeDtypeStruct((key_matrix.shape[0] // 2, span), tokens.dtype)
    vmem = pl.BlockSpec(memory_space=pltpu.VMEM)
    return pl.pallas_call(
        functools.partial(cut_kernel, kv),
        in_specs=[pl.BlockSpec(memory_space=pltpu.SMEM)] + [pl.BlockSpec(memory_space=pl.ANY)] * 4,
        out_specs=[vmem] * (1 + len(halves)),
        out_shape=halves + [send],
        scratch_shapes=[pltpu.SemaphoreType.DMA((3 + len(halves),))],
        compiler_params=pltpu.CompilerParams(vmem_limit_bytes=60 * 2**20),
        cost_estimate=pl.CostEstimate(flops=0, bytes_accessed=0, transcendentals=0),
    )(place, tokens, key_matrix, value_matrix, query_matrix)


def sums_kernel(count, blocks, place_ref, *refs):
    pieces, (weights_ref, theirs_ref, others_ref), outs = refs[: 2 * count], refs[2 * count : 2 * count + 3], refs[2 * count + 3 : -1]
    feats_ref = refs[-1]
    first_core, group = place_ref[1], place_ref[2]
    share, half = pieces[0].shape[0] // blocks, theirs_ref.shape[0]
    for i in range(count):
        start = 0 if count == 1 else (place_ref[0] if i == 0 else 1 - place_ref[0]) * share
        for block in range(blocks):
            rows = pl.ds(pl.multiple_of(block * count * share + start, 64), share)
            cut_rows = slice(block * share, (block + 1) * share)
            feats_ref[1 - first_core, rows, :] = pieces[2 * i][cut_rows, :]
            feats_ref[first_core, rows, :] = pieces[2 * i + 1][cut_rows, :]
    here = pl.ds(pl.multiple_of(group * half, HEAD_DIM), half)
    there = pl.ds(pl.multiple_of((1 - group) * half, HEAD_DIM), half)
    span = outs[0].shape[1]
    step = 2 * HEAD_DIM
    first = 0
    for out_ref in outs:
        rows = slice(first, first + out_ref.shape[0])
        first += out_ref.shape[0]
        for col in range(0, span, step):
            cols = slice(col, min(span, col + step))
            total = jnp.dot(feats_ref[0, rows], weights_ref[:, cols], preferred_element_type=jnp.float32)
            total += jnp.dot(feats_ref[1, rows, here], theirs_ref[:, cols], preferred_element_type=jnp.float32)
            total += jnp.dot(feats_ref[1, rows, there], others_ref[:, cols], preferred_element_type=jnp.float32)
            out_ref[:, cols] = total.astype(out_ref.dtype)


def sums(name, place, pieces, blocks, outs, weights, theirs, others, dtype):
    count = len(pieces) // 2
    rows, feats = count * pieces[0].shape[0], pieces[0].shape[1]
    span = weights.shape[1]
    vmem = pl.BlockSpec(memory_space=pltpu.VMEM)
    with jax.named_scope(name):
        return pl.pallas_call(
            functools.partial(sums_kernel, count, blocks),
            in_specs=[pl.BlockSpec(memory_space=pltpu.SMEM)] + [vmem] * (2 * count + 3),
            out_specs=[vmem] * outs,
            out_shape=[jax.ShapeDtypeStruct((rows // outs, span), dtype)] * outs,
            scratch_shapes=[pltpu.VMEM((2, rows, feats), jnp.bfloat16)],
            compiler_params=pltpu.CompilerParams(vmem_limit_bytes=32 * 2**20),
            cost_estimate=pl.CostEstimate(flops=0, bytes_accessed=0, transcendentals=0),
        )(place, *pieces, weights, theirs, others)


def slot_hits(holder, row_slot, width):
    lane = lax.broadcasted_iota(jnp.int32, (row_slot.shape[0], width), 1)
    return row_slot == holder * 2 + (lane >= width // 2).astype(jnp.int32)


def held_maps(inner, maps, rows):
    last = [jnp.where(inner == 1, maps[i][rows], maps[i + 1][rows]) for i in (2, 4)]
    return [maps[0][rows], maps[1][rows], *last]


def shrink_kernel(holder_ref, slot_ref, tok_ref, *refs):
    out_ref = refs[-1]
    feats, width = tok_ref.shape[1], refs[0].shape[1]
    total = jnp.zeros((tok_ref.shape[0], width), jnp.float32)
    for k, down in enumerate(held_maps(holder_ref[4], refs[:-1], slice(0, feats))):
        product = jnp.dot(tok_ref[...], down, preferred_element_type=jnp.float32)
        total += jnp.where(slot_hits(holder_ref[k], slot_ref[...], width), product, 0.0)
    out_ref[...] = total[:, : width // 2] + total[:, width // 2 :]


def expand_kernel(feats, holder_ref, slot_ref, own_ref, cores_ref, chips_ref, both_ref, *refs):
    out_ref = refs[-1]
    width = refs[0].shape[1]
    low_rank = (own_ref[...] + cores_ref[...]) + (chips_ref[...] + both_ref[...])
    low_rank = low_rank.astype(jnp.bfloat16)
    twice = jnp.concatenate([low_rank, low_rank], axis=1)
    total = jnp.zeros(out_ref.shape, jnp.float32)
    for k, up in enumerate(held_maps(holder_ref[4], refs[:-1], slice(feats, refs[0].shape[0]))):
        spread = jnp.where(slot_hits(holder_ref[k], slot_ref[...], width), twice, jnp.zeros_like(twice))
        total += lax.dot_general(spread, up, (((1,), (1,)), ((), ())), preferred_element_type=jnp.float32)
    out_ref[...] = total.astype(out_ref.dtype)


def adapter_call(name, kernel, shape, holders, *operands):
    vmem = pl.BlockSpec(memory_space=pltpu.VMEM)
    with jax.named_scope(name):
        return pl.pallas_call(
            kernel,
            in_specs=[pl.BlockSpec(memory_space=pltpu.SMEM)] + [vmem] * len(operands),
            out_specs=vmem,
            out_shape=shape,
            compiler_params=pltpu.CompilerParams(vmem_limit_bytes=24 * 2**20),
            cost_estimate=pl.CostEstimate(flops=0, bytes_accessed=0, transcendentals=0),
        )(holders, *operands)


PAIRED = (4, 4, 2)
FAR = [(0, 2), (3, 1)]
INNER = [(1, 2), (2, 1), (0, 0), (3, 3)]
OUTWARD = [(1, 0), (2, 3), (0, 1), (3, 2)]


def shards_paired(
    tokens,
    query_matrix,
    key_matrix,
    value_matrix,
    query_down_maps,
    query_up_maps,
    request_lengths,
    request_adapter,
    adapter_pool_slot,
):
    pools, parts, groups = PAIRED
    tok_count, feat_count = tokens.shape
    req_count = request_lengths.shape[1]
    adapter_count = adapter_pool_slot.shape[0]
    slots_own, _, rank = query_down_maps.shape
    group, pool, part = lax.axis_index("groups"), lax.axis_index("pool"), lax.axis_index("tp")
    f32, bf16 = jnp.float32, jnp.bfloat16
    dot = functools.partial(jnp.dot, preferred_element_type=f32)
    here = part // 2 == pool // 2
    first_core = pool % 2 == part % 2
    place = jnp.stack([here.astype(jnp.int32), first_core.astype(jnp.int32), group.astype(jnp.int32), (pool % 3 > 0).astype(jnp.int32)])

    def permute(name, x, axes, pairs):
        with jax.named_scope(name):
            return lax.ppermute(x, axes, pairs)

    def chip_swap(name, x, bits=2):
        return permute(name, x, "tp", [(t, t ^ bits) for t in range(parts)])

    def core_swap(name, x):
        return chip_swap(name, x, 1)

    def after(x, *done):
        return lax.optimization_barrier((x,) + done)[0]

    kv_count = key_matrix.shape[1] // HEAD_DIM
    wide = query_matrix.shape[1] // kv_count
    in_pairs = [(i, i ^ 1) for i in range(pools)]
    replicas = [(g * pools + p, (1 - g) * pools + p) for g in range(groups) for p in range(pools)]
    top, bottom, send = cut(0, place, tokens, key_matrix, value_matrix, query_matrix)

    request = request_local(request_lengths[0], tok_count)
    slot_table = jnp.sum(
        jnp.where(
            request_adapter[:, 0][:, None] == jnp.arange(adapter_count)[None, :],
            adapter_pool_slot[None, :],
            0,
        ),
        axis=1,
        dtype=jnp.int32,
    )
    row_slot = jnp.sum(
        jnp.where(request[:, None] == jnp.arange(req_count)[None, :], slot_table[None, :], 0),
        axis=1,
        dtype=jnp.int32,
    )
    bias = request_bias(request)

    top_here = chip_swap("tokens_top", top)
    first = permute("weights_0", send, "pool", in_pairs)
    maps = jnp.concatenate(
        [query_down_maps[i] for i in range(slots_own)], axis=1
    ), query_up_maps.reshape(slots_own * rank, -1).T
    maps = after(jnp.concatenate(maps, axis=0), top)
    leaving = jnp.where(here, after(top_here, maps, row_slot, bias), bottom)
    far = permute("tokens_far", leaving, "pool", FAR)
    (send,) = cut(1, after(place, leaving), tokens, key_matrix, value_matrix, query_matrix)
    late = lax.optimization_barrier((key_matrix, value_matrix, query_matrix, leaving))
    weights = [
        jnp.concatenate(
            [
                late[0][:, kv * HEAD_DIM : (kv + 1) * HEAD_DIM],
                late[1][:, kv * HEAD_DIM : (kv + 1) * HEAD_DIM],
                late[2][:, kv * wide : (kv + 1) * wide],
            ],
            axis=1,
        )
        for kv in range(kv_count)
    ]
    near = permute("tokens_near", leaving, "pool", INNER)

    pair_maps = permute("maps_pair", after(maps, first), "pool", in_pairs)
    maps = after(maps, far)
    others = [permute("weights_0_replicas", after(first, send, *weights), ("groups", "pool"), replicas)]
    theirs = [first, permute("weights_1", after(send, pair_maps), "pool", in_pairs)]
    others.append(permute("weights_1_replicas", theirs[1], ("groups", "pool"), replicas))
    far_chips = chip_swap("far_chips", after(far, first, near))
    inner_maps = permute("maps_inner", maps, "pool", INNER)
    outer_maps = permute("maps_outer", pair_maps, "pool", INNER)
    far_pieces = (
        far,
        core_swap("far_cores_a", far),
        far_chips,
        core_swap("far_cores_b", after(far_chips, others[0], inner_maps)),
    )
    near_chips = chip_swap("near_chips", after(near, far_chips))
    near_pieces = near, core_swap("near_cores_a", near), near_chips, core_swap("near_cores_b", near_chips)
    inner_out = permute("maps_inner_out", after(inner_maps, theirs[1]), "pool", OUTWARD)
    outer_out = permute("maps_outer_out", after(outer_maps, theirs[1]), "pool", OUTWARD)
    bottom_here = permute(
        "tokens_bottom",
        after(bottom, near_chips),
        ("pool", "tp"),
        [(p * parts + t, p * parts + (t ^ 2)) for p in range(pools) for t in range(parts) if t // 2 == p // 2],
    )
    mine = jnp.where(here, tokens, jnp.concatenate([top_here, bottom_here], axis=0))
    own_pieces = mine, core_swap("own_cores", mine)

    def part_sums(name, kv, pieces, dtype, earlier=()):
        both = weights[kv], theirs[kv], others[kv]
        return sums(f"{name}_{kv}", after(place, *earlier), pieces, 1, 1, *both, dtype)[0]

    far_0 = part_sums("far", 0, far_pieces, bf16)
    arrived_far = [permute("sums_far_0", far_0, "pool", INNER)]
    near_0 = part_sums("near", 0, near_pieces, bf16, (far_0, outer_maps))
    arrived_near = [permute("sums_near_0", after(near_0, arrived_far[0]), "pool", INNER)]
    own_0 = part_sums("own", 0, own_pieces, f32, (near_0,))
    far_1 = part_sums("far", 1, far_pieces, bf16, (own_0, inner_out))
    arrived_far.append(permute("sums_far_1", after(far_1, arrived_near[0]), "pool", INNER))
    forwarded = [permute("sums_out_0", arrived_far[0], "pool", OUTWARD)]
    own = [own_0, part_sums("own", 1, own_pieces, f32, (far_1,))]

    inner = 2 - pool // 2
    holders = jnp.stack([pool, pool ^ 1, inner, inner ^ 1, place[3]]).astype(jnp.int32)
    held = maps, pair_maps, inner_maps, inner_out, outer_maps, outer_out
    slots = row_slot[:, None]
    shrunk = adapter_call(
        "low_rank", shrink_kernel, jax.ShapeDtypeStruct((tok_count, rank), f32), holders, slots, after(tokens, far_1), *held
    )
    near_1 = part_sums("near", 1, near_pieces, bf16, (own[1], shrunk))
    arrived_near.append(permute("sums_near_1", after(near_1, arrived_far[1], forwarded[0]), "pool", INNER))
    forwarded.append(permute("sums_out_1", arrived_far[1], "pool", OUTWARD))

    delta = adapter_call(
        "delta",
        functools.partial(expand_kernel, feat_count),
        jax.ShapeDtypeStruct((tok_count, query_matrix.shape[1]), bf16),
        holders,
        slots,
        shrunk,
        core_swap("low_rank_cores", shrunk),
        chip_swap("low_rank_chips", shrunk),
        chip_swap("low_rank_both", shrunk, 3),
        *held,
    )
    mixed = None
    for kv in range(kv_count):
        mixed = attend_head(kv, kv_count, place, own[kv], arrived_near[kv], forwarded[kv], delta, bias, mixed)
    return mixed


def solution(mesh):
    placed = (
        P(("groups", "pool"), "tp"),
        P("pool", "tp"),
        P("pool", "tp"),
        P("pool", "tp"),
        P(("groups", "pool"), "tp", None),
        P(("groups", "pool"), None, "tp"),
        P(("groups", "pool"), None),
        P(("groups", "pool"), None),
        P(),
    )
    sizes = mesh.shape
    if (sizes["pool"], sizes["tp"], sizes["groups"]) == PAIRED:
        shards = shards_paired
    else:
        shards = shards_gathered
    return jax.shard_map(
        shards, mesh=mesh, in_specs=placed, out_specs=P(("groups", "pool"), "tp"), check_vma=False
    )
```

```python
import functools

import jax
import jax.numpy as jnp
from jax import lax
from jax.experimental import pallas as pl
from jax.experimental.pallas import tpu as pltpu
from jax.sharding import PartitionSpec as P

HEAD_DIM = 128
LEN_MOST = 16


def request_local(lengths_row, tok_count):
    boundary = jnp.cumsum(lengths_row, dtype=jnp.int32)
    position = jnp.arange(tok_count, dtype=jnp.int32)
    return jnp.sum(
        (position[:, None] >= boundary[None, :]).astype(jnp.int32), axis=1, dtype=jnp.int32
    )


def attend_local(queries, key_vals, value_vals, request, head_dim):
    tok_count = queries.shape[0]
    kv_count = key_vals.shape[1] // head_dim
    group_size = queries.shape[1] // key_vals.shape[1]
    query_h = queries.reshape(tok_count, kv_count, group_size, head_dim)
    key_h = key_vals.reshape(tok_count, kv_count, head_dim)
    value_h = value_vals.reshape(tok_count, kv_count, head_dim)
    scores = jnp.einsum(
        "tkgd,skd->kgts", query_h, key_h, preferred_element_type=jnp.float32
    ) * head_dim ** (-0.5)
    position = jnp.arange(tok_count)
    allowed = (request[:, None] == request[None, :]) & (position[None, :] <= position[:, None])
    scores = jnp.where(allowed, scores, -1e30)
    top_score = jnp.max(scores, axis=-1, keepdims=True)
    exp_terms = jnp.exp(scores - top_score)
    softmax_w = (exp_terms / jnp.sum(exp_terms, axis=-1, keepdims=True)).astype(jnp.bfloat16)
    mixed = jnp.einsum("kgts,skd->tkgd", softmax_w, value_h, preferred_element_type=jnp.float32)
    return mixed.astype(jnp.bfloat16).reshape(tok_count, kv_count * group_size * head_dim)


def shards_gathered(
    tokens,
    query_matrix,
    key_matrix,
    value_matrix,
    query_down_maps,
    query_up_maps,
    request_lengths,
    request_adapter,
    adapter_pool_slot,
):
    tok_count = tokens.shape[0]
    feat_count = tokens.shape[1]
    req_count = request_lengths.shape[1]
    adapter_count = adapter_pool_slot.shape[0]
    capacity = max(2, req_count // adapter_count) * LEN_MOST
    request = request_local(request_lengths[0], tok_count)
    slot_table = jnp.sum(
        jnp.where(
            request_adapter[:, 0][:, None] == jnp.arange(adapter_count)[None, :],
            adapter_pool_slot[None, :],
            0,
        ),
        axis=1,
        dtype=jnp.int32,
    )
    row_slot = jnp.sum(
        jnp.where(request[:, None] == jnp.arange(req_count)[None, :], slot_table[None, :], 0),
        axis=1,
        dtype=jnp.int32,
    )
    slot_hit = (row_slot[:, None] == jnp.arange(adapter_count)[None, :]).astype(jnp.int32)
    earlier = jnp.cumsum(slot_hit, axis=0, dtype=jnp.int32) - slot_hit
    target = row_slot * capacity + jnp.sum(earlier * slot_hit, axis=1, dtype=jnp.int32)
    packed = jnp.zeros((adapter_count * capacity, feat_count), jnp.bfloat16).at[target].set(tokens)
    packed = packed.reshape(adapter_count, capacity, feat_count)
    tok_full = lax.all_gather(tokens, "tp", axis=1, tiled=True)
    pieces = (
        lax.all_gather(query_matrix, "pool", axis=0, tiled=True),
        lax.all_gather(key_matrix, "pool", axis=0, tiled=True),
        lax.all_gather(value_matrix, "pool", axis=0, tiled=True),
    )
    query_base, key_raw, value_raw = tuple(
        (
            jnp.dot(tok_full, weight_piece, preferred_element_type=jnp.float32)
            for weight_piece in pieces
        )
    )
    shrunk = jnp.einsum(
        "sjd,sdr->sjr",
        packed,
        lax.all_gather(query_down_maps, "pool", axis=0, tiled=True),
        preferred_element_type=jnp.float32,
    )
    low_rank = lax.psum(shrunk, "tp").astype(jnp.bfloat16)
    delta = jnp.einsum(
        "sjr,srk->sjk",
        low_rank,
        lax.all_gather(query_up_maps, "pool", axis=0, tiled=True),
        preferred_element_type=jnp.float32,
    ).astype(jnp.bfloat16)
    delta_tokens = delta.reshape(adapter_count * capacity, delta.shape[2])[target]
    queries = (query_base + delta_tokens.astype(jnp.float32)).astype(jnp.bfloat16)
    return attend_local(
        queries, key_raw.astype(jnp.bfloat16), value_raw.astype(jnp.bfloat16), request, HEAD_DIM
    )


UNIT = 128


def attend_kernel(group_size, place_ref, own_ref, near_ref, far_ref, delta_ref, bias_ref, *refs):
    out_ref, sum_ref = refs[-2:]
    wide = own_ref[...] + jnp.where(place_ref[3] == 1, near_ref[...], far_ref[...]).astype(jnp.float32)
    sum_ref[:, : 2 * HEAD_DIM] = wide[:, : 2 * HEAD_DIM].astype(jnp.bfloat16)
    sum_ref[:, 2 * HEAD_DIM :] = (wide[:, 2 * HEAD_DIM :] + delta_ref[...].astype(jnp.float32)).astype(jnp.bfloat16)
    for b in range(own_ref.shape[0] // UNIT):
        rows = slice(b * UNIT, (b + 1) * UNIT)
        keys = slice(max(0, b - 1) * UNIT, (b + 1) * UNIT)
        bias = bias_ref[b] if b > 0 else bias_ref[b][:, UNIT:]
        query = jnp.concatenate(
            [sum_ref[rows, (2 + i) * HEAD_DIM : (3 + i) * HEAD_DIM] for i in range(group_size)], axis=0
        )
        scores = lax.dot_general(
            query, sum_ref[keys, :HEAD_DIM], (((1,), (1,)), ((), ())), preferred_element_type=jnp.float32
        ) * HEAD_DIM ** (-0.5)
        scores = scores + jnp.concatenate([bias] * group_size, axis=0)
        exp_terms = jnp.exp(scores - jnp.max(scores, axis=-1, keepdims=True))
        weights = (exp_terms / jnp.sum(exp_terms, axis=-1, keepdims=True)).astype(jnp.bfloat16)
        mixed = jnp.dot(
            weights, sum_ref[keys, HEAD_DIM : 2 * HEAD_DIM], preferred_element_type=jnp.float32
        ).astype(jnp.bfloat16)
        for i in range(group_size):
            out_ref[rows, i * HEAD_DIM : (i + 1) * HEAD_DIM] = mixed[i * UNIT : (i + 1) * UNIT]


def attend_head(kv, kv_count, place, own, near, far, delta, bias, earlier):
    rows, span = own.shape
    group_size = span // HEAD_DIM - 2
    wide = group_size * HEAD_DIM
    whole = [pl.BlockSpec((rows, span), lambda i, b=x.shape[0] // rows - 1: (b, 0)) for x in (own, near, far)]
    specs = [pl.BlockSpec(memory_space=pltpu.SMEM)] + whole + [pl.BlockSpec((rows, wide), lambda i: (0, kv)), pl.BlockSpec(bias.shape, lambda i: (0, 0, 0))]
    operands = [place, own, near, far, delta, bias]
    aliases = {}
    if earlier is not None:
        specs.append(pl.BlockSpec(memory_space=pl.ANY))
        operands.append(earlier)
        aliases = {6: 0}
    return pl.pallas_call(
        functools.partial(attend_kernel, group_size),
        grid=(1,),
        in_specs=specs,
        out_specs=pl.BlockSpec((rows, wide), lambda i: (0, kv)),
        out_shape=jax.ShapeDtypeStruct((rows, kv_count * wide), jnp.bfloat16),
        scratch_shapes=[pltpu.VMEM((rows, span), jnp.bfloat16)],
        input_output_aliases=aliases,
        compiler_params=pltpu.CompilerParams(vmem_limit_bytes=12 * 2**20),
        cost_estimate=pl.CostEstimate(flops=0, bytes_accessed=0, transcendentals=0),
    )(*operands)


def request_bias(request):
    blocks = request.shape[0] // UNIT
    padded = jnp.concatenate([jnp.full((UNIT,), -1, jnp.int32), request])
    keys = jnp.stack([padded[b * UNIT : (b + 2) * UNIT] for b in range(blocks)])
    row = jnp.arange(UNIT)[:, None]
    col = jnp.arange(2 * UNIT)[None, :]
    allowed = (request.reshape(blocks, UNIT, 1) == keys[:, None, :]) & (col <= row + UNIT)[None]
    return jnp.where(allowed, 0.0, -1e30).astype(jnp.float32)


def copy_all(pairs, sems):
    copies = [pltpu.make_async_copy(*pair, sems.at[i]) for i, pair in enumerate(pairs)]
    for copy in copies:
        copy.start()
    for copy in copies:
        copy.wait()


def halves_kernel(tok_ref, top_ref, bottom_ref, sems):
    rows = top_ref.shape[0]
    copy_all([(tok_ref.at[pl.ds(i * rows, rows)], ref) for i, ref in enumerate((top_ref, bottom_ref))], sems)


def cut_kernel(parts, place_ref, key_ref, value_ref, query_ref, *refs):
    pairs = []
    for (kv, sent), out_ref in zip(parts, refs[:-1]):
        count, wide = out_ref.shape[0], out_ref.shape[1] - 2 * HEAD_DIM
        rows = pl.ds(pl.multiple_of(place_ref[2] * count, 64), count) if sent else pl.ds(0, count)
        small = pl.ds(kv * HEAD_DIM, HEAD_DIM)
        pairs.append((key_ref.at[rows, small], out_ref.at[:, pl.ds(0, HEAD_DIM)]))
        pairs.append((value_ref.at[rows, small], out_ref.at[:, pl.ds(HEAD_DIM, HEAD_DIM)]))
        pairs.append((query_ref.at[rows, pl.ds(kv * wide, wide)], out_ref.at[:, pl.ds(2 * HEAD_DIM, wide)]))
    copy_all(pairs, refs[-1])


def copying(kernel, prefetch, operands, outs, copies, grant=60):
    smem = [pl.BlockSpec(memory_space=pltpu.SMEM)] * len(prefetch)
    vmem = pl.BlockSpec(memory_space=pltpu.VMEM)
    return pl.pallas_call(
        kernel,
        in_specs=smem + [pl.BlockSpec(memory_space=pl.ANY)] * len(operands),
        out_specs=[vmem] * len(outs),
        out_shape=outs,
        scratch_shapes=[pltpu.SemaphoreType.DMA((copies,))],
        compiler_params=pltpu.CompilerParams(vmem_limit_bytes=grant * 2**20),
        cost_estimate=pl.CostEstimate(flops=0, bytes_accessed=0, transcendentals=0),
    )(*prefetch, *operands)


def halves(tokens):
    out = jax.ShapeDtypeStruct((tokens.shape[0] // 2, tokens.shape[1]), tokens.dtype)
    return copying(halves_kernel, (), (tokens,), [out, out], 2)


def cut(parts, place, key_matrix, value_matrix, query_matrix):
    feats, narrow = key_matrix.shape
    span = 2 * HEAD_DIM + query_matrix.shape[1] * HEAD_DIM // narrow
    outs = [jax.ShapeDtypeStruct((feats // 2 if sent else feats, span), key_matrix.dtype) for _, sent in parts]
    kernel = functools.partial(cut_kernel, parts)
    grant = 60 if len(parts) == 1 else 24
    return copying(kernel, (place,), (key_matrix, value_matrix, query_matrix), outs, 3 * len(parts), grant)


def sums_kernel(layout, place_ref, *refs):
    weights_ref, theirs_ref, others_ref, out_ref, feats_ref = refs[-5:]
    first_core, group = place_ref[1], place_ref[2]
    share, half = feats_ref.shape[1] // len(layout), theirs_ref.shape[0]
    rest = list(refs[:-5])
    for i, counts in enumerate(layout):
        start = 0 if len(layout) == 1 else (place_ref[0] if i == 0 else 1 - place_ref[0]) * share
        for block, count in zip((1 - first_core, first_core), counts):
            done = 0
            for piece_ref in [rest.pop(0) for _ in range(count)]:
                rows = pl.ds(pl.multiple_of(start + done, 32), piece_ref.shape[0])
                feats_ref[block, rows, :] = piece_ref[...]
                done += piece_ref.shape[0]
    here = pl.ds(pl.multiple_of(group * half, HEAD_DIM), half)
    there = pl.ds(pl.multiple_of((1 - group) * half, HEAD_DIM), half)
    span = out_ref.shape[1]
    step = 2 * HEAD_DIM
    for col in range(0, span, step):
        cols = slice(col, min(span, col + step))
        total = jnp.dot(feats_ref[0], weights_ref[:, cols], preferred_element_type=jnp.float32)
        total += jnp.dot(feats_ref[1, :, here], theirs_ref[:, cols], preferred_element_type=jnp.float32)
        total += jnp.dot(feats_ref[1, :, there], others_ref[:, cols], preferred_element_type=jnp.float32)
        out_ref[:, cols] = total.astype(out_ref.dtype)


def sums(name, place, shares, weights, theirs, others, dtype):
    layout = [tuple(len(pieces) for pieces in share) for share in shares]
    pieces = [x for share in shares for part in share for x in part]
    rows, feats = sum(x.shape[0] for share in shares for x in share[0]), weights.shape[0]
    span = weights.shape[1]
    vmem = pl.BlockSpec(memory_space=pltpu.VMEM)
    with jax.named_scope(name):
        return pl.pallas_call(
            functools.partial(sums_kernel, layout),
            in_specs=[pl.BlockSpec(memory_space=pltpu.SMEM)] + [vmem] * (len(pieces) + 3),
            out_specs=vmem,
            out_shape=jax.ShapeDtypeStruct((rows, span), dtype),
            scratch_shapes=[pltpu.VMEM((2, rows, feats), jnp.bfloat16)],
            compiler_params=pltpu.CompilerParams(vmem_limit_bytes=12 * 2**20),
            cost_estimate=pl.CostEstimate(flops=0, bytes_accessed=0, transcendentals=0),
        )(place, *pieces, weights, theirs, others)


def slot_hits(holder, row_slot, width):
    lane = lax.broadcasted_iota(jnp.int32, (row_slot.shape[0], width), 1)
    return row_slot == holder * 2 + (lane >= width // 2).astype(jnp.int32)


def held_maps(inner, maps, first, buffers, sems):
    rows = buffers.shape[1]
    copy_all([(x.at[pl.ds(first, rows)], buffers.at[i]) for i, x in enumerate(maps)], sems)
    return [buffers[0], buffers[1], buffers[3 - inner], buffers[5 - inner]]


def shrink_kernel(holder_ref, slot_ref, tok_ref, *refs):
    out_ref, buffers, sems = refs[-3:]
    width = buffers.shape[2]
    total = jnp.zeros((tok_ref.shape[0], width), jnp.float32)
    for k, down in enumerate(held_maps(holder_ref[4], refs[:-3], 0, buffers, sems)):
        product = jnp.dot(tok_ref[...], down, preferred_element_type=jnp.float32)
        total += jnp.where(slot_hits(holder_ref[k], slot_ref[...], width), product, 0.0)
    out_ref[...] = total[:, : width // 2] + total[:, width // 2 :]


def expand_kernel(holder_ref, slot_ref, own_ref, cores_ref, chips_ref, both_ref, *refs):
    out_ref, buffers, sems = refs[-3:]
    width = buffers.shape[2]
    maps = held_maps(holder_ref[4], refs[:-3], refs[0].shape[0] - buffers.shape[1], buffers, sems)
    low_rank = (own_ref[...] + cores_ref[...]) + (chips_ref[...] + both_ref[...])
    low_rank = low_rank.astype(jnp.bfloat16)
    twice = jnp.concatenate([low_rank, low_rank], axis=1)
    total = jnp.zeros(out_ref.shape, jnp.float32)
    for k, up in enumerate(maps):
        spread = jnp.where(slot_hits(holder_ref[k], slot_ref[...], width), twice, jnp.zeros_like(twice))
        total += lax.dot_general(spread, up, (((1,), (1,)), ((), ())), preferred_element_type=jnp.float32)
    out_ref[...] = total.astype(out_ref.dtype)


def adapter_call(name, kernel, shape, rows, holders, operands, maps):
    vmem = pl.BlockSpec(memory_space=pltpu.VMEM)
    with jax.named_scope(name):
        return pl.pallas_call(
            kernel,
            in_specs=[pl.BlockSpec(memory_space=pltpu.SMEM)]
            + [vmem] * len(operands)
            + [pl.BlockSpec(memory_space=pl.ANY)] * len(maps),
            out_specs=vmem,
            out_shape=shape,
            scratch_shapes=[
                pltpu.VMEM((len(maps), rows, maps[0].shape[1]), maps[0].dtype),
                pltpu.SemaphoreType.DMA((len(maps),)),
            ],
            compiler_params=pltpu.CompilerParams(vmem_limit_bytes=12 * 2**20),
            cost_estimate=pl.CostEstimate(flops=0, bytes_accessed=0, transcendentals=0),
        )(holders, *operands, *maps)


PAIRED = (4, 4, 2)
FAR = [(0, 2), (3, 1)]
INNER = [(1, 2), (2, 1), (0, 0), (3, 3)]
OUTWARD = [(1, 0), (2, 3), (0, 1), (3, 2)]


def shards_paired(
    tokens,
    query_matrix,
    key_matrix,
    value_matrix,
    query_down_maps,
    query_up_maps,
    request_lengths,
    request_adapter,
    adapter_pool_slot,
):
    pools, parts, groups = PAIRED
    tok_count, feat_count = tokens.shape
    req_count = request_lengths.shape[1]
    adapter_count = adapter_pool_slot.shape[0]
    slots_own, _, rank = query_down_maps.shape
    group, pool, part = lax.axis_index("groups"), lax.axis_index("pool"), lax.axis_index("tp")
    f32, bf16 = jnp.float32, jnp.bfloat16
    dot = functools.partial(jnp.dot, preferred_element_type=f32)
    here = part // 2 == pool // 2
    first_core = pool % 2 == part % 2
    place = jnp.stack([here.astype(jnp.int32), first_core.astype(jnp.int32), group.astype(jnp.int32), (pool % 3 > 0).astype(jnp.int32)])

    def permute(name, x, axes, pairs):
        with jax.named_scope(name):
            return lax.ppermute(x, axes, pairs)

    def chip_swap(name, x, bits=2):
        return permute(name, x, "tp", [(t, t ^ bits) for t in range(parts)])

    def core_swap(name, x):
        return chip_swap(name, x, 1)

    def after(x, *done):
        return lax.optimization_barrier((x,) + done)[0]

    kv_count = key_matrix.shape[1] // HEAD_DIM
    wide = query_matrix.shape[1] // kv_count
    in_pairs = [(i, i ^ 1) for i in range(pools)]
    replicas = [(g * pools + p, (1 - g) * pools + p) for g in range(groups) for p in range(pools)]
    matrices = key_matrix, value_matrix, query_matrix
    half_rows = tok_count // 2
    (first_send,) = cut([(0, True)], place, *matrices)
    top, bottom = halves(after(tokens, first_send))

    request = request_local(request_lengths[0], tok_count)
    slot_table = jnp.sum(
        jnp.where(
            request_adapter[:, 0][:, None] == jnp.arange(adapter_count)[None, :],
            adapter_pool_slot[None, :],
            0,
        ),
        axis=1,
        dtype=jnp.int32,
    )
    row_slot = jnp.sum(
        jnp.where(request[:, None] == jnp.arange(req_count)[None, :], slot_table[None, :], 0),
        axis=1,
        dtype=jnp.int32,
    )
    bias = request_bias(request)

    top_here = chip_swap("tokens_top", top)
    first = permute("weights_0", first_send, "pool", in_pairs)
    maps = jnp.concatenate(
        [query_down_maps[i] for i in range(slots_own)], axis=1
    ), query_up_maps.reshape(slots_own * rank, -1).T
    maps = after(jnp.concatenate(maps, axis=0), top)
    inner_maps = permute("maps_inner", maps, "pool", INNER)
    leaving = jnp.where(here, after(top_here, maps, row_slot, bias), bottom)
    far = permute("tokens_far", leaving, "pool", FAR)
    later = [(kv, True) for kv in range(1, kv_count)] + [(kv, False) for kv in range(kv_count)]
    send, *weights = cut(later, after(place, leaving), *matrices)
    near = permute("tokens_near", after(leaving, far), "pool", INNER)

    pair_maps = permute("maps_pair", after(maps, first), "pool", in_pairs)
    bottom_here = chip_swap("tokens_bottom", after(bottom, leaving))
    mine = jnp.where(here, tokens, jnp.concatenate([top_here, bottom_here], axis=0))
    own_cores = core_swap("own_cores", mine)
    others = [permute("weights_0_replicas", after(first, send, *weights, bottom_here, inner_maps), ("groups", "pool"), replicas)]
    theirs = [first, permute("weights_1", after(send, pair_maps), "pool", in_pairs)]
    others.append(permute("weights_1_replicas", theirs[1], ("groups", "pool"), replicas))
    far_chips = chip_swap("far_chips", far)
    outer_maps = permute("maps_outer", pair_maps, "pool", INNER)
    far_cores = core_swap("far_cores_a", far), core_swap("far_cores_b", after(far_chips, others[0], pair_maps, own_cores))
    far_pieces = [([far], far_cores[:1]), ([far_chips], far_cores[1:])]
    near_chips = chip_swap("near_chips", after(near, far_chips))
    inner_out = permute("maps_inner_out", after(inner_maps, theirs[1]), "pool", OUTWARD)
    outer_out = permute("maps_outer_out", after(outer_maps, theirs[1]), "pool", OUTWARD)
    def part_sums(name, kv, pieces, dtype, earlier=()):
        both = weights[kv], theirs[kv], others[kv]
        return sums(f"{name}_{kv}", after(place, *earlier), pieces, *both, dtype)

    far_0 = part_sums("far", 0, far_pieces, bf16)
    arrived_far = [permute("sums_far_0", far_0, "pool", INNER)]
    near_cores = core_swap("near_cores_a", near)
    fine = half_rows // 2
    near_fine = [core_swap(f"near_cores_b{i}", near_chips[i * fine : (i + 1) * fine]) for i in range(2)]
    near_pieces = [([near], [near_cores]), ([near_chips], near_fine)]
    near_0 = part_sums("near", 0, near_pieces, bf16, (far_0, outer_maps))
    arrived_near = [permute("sums_near_0", after(near_0, arrived_far[0]), "pool", INNER)]
    own_pieces = [([mine], [own_cores])]
    own_0 = part_sums("own", 0, own_pieces, f32, (near_0,))
    far_1 = part_sums("far", 1, far_pieces, bf16, (own_0, inner_out))
    arrived_far.append(permute("sums_far_1", after(far_1, arrived_near[0], arrived_far[0]), "pool", INNER))
    forwarded = [permute("sums_out_0", arrived_far[0], "pool", OUTWARD)]
    own = [own_0, part_sums("own", 1, own_pieces, f32, (far_1,))]

    inner = 2 - pool // 2
    holders = jnp.stack([pool, pool ^ 1, inner, inner ^ 1, place[3]]).astype(jnp.int32)
    held = maps, pair_maps, inner_maps, inner_out, outer_maps, outer_out
    slots = row_slot[:, None]
    shrunk = jax.ShapeDtypeStruct((tok_count, rank), f32)
    shrunk = adapter_call(
        "low_rank", shrink_kernel, shrunk, feat_count, holders, (slots, after(tokens, near_0)), held
    )
    shares = [shrunk] + [chip_swap(f"low_rank_{bits}", shrunk, bits) for bits in range(1, parts)]
    near_1 = part_sums("near", 1, near_pieces, bf16, (own[1], shrunk))
    arrived_near.append(permute("sums_near_1", after(near_1, arrived_far[1], forwarded[0]), "pool", INNER))
    forwarded.append(permute("sums_out_1", arrived_far[1], "pool", OUTWARD))
    delta = jax.ShapeDtypeStruct((tok_count, query_matrix.shape[1]), bf16)
    delta = adapter_call(
        "delta", expand_kernel, delta, maps.shape[0] - feat_count, holders, (slots, *shares), held
    )
    mixed = None
    for kv in range(kv_count):
        mixed = attend_head(kv, kv_count, place, own[kv], arrived_near[kv], forwarded[kv], delta, bias, mixed)
    return mixed


def solution(mesh):
    placed = (
        P(("groups", "pool"), "tp"),
        P("pool", "tp"),
        P("pool", "tp"),
        P("pool", "tp"),
        P(("groups", "pool"), "tp", None),
        P(("groups", "pool"), None, "tp"),
        P(("groups", "pool"), None),
        P(("groups", "pool"), None),
        P(),
    )
    sizes = mesh.shape
    if (sizes["pool"], sizes["tp"], sizes["groups"]) == PAIRED:
        shards = shards_paired
    else:
        shards = shards_gathered
    return jax.shard_map(
        shards, mesh=mesh, in_specs=placed, out_specs=P(("groups", "pool"), "tp"), check_vma=False
    )
```

```python
import functools

import jax
import jax.numpy as jnp
from jax import lax
from jax.experimental import pallas as pl
from jax.experimental.pallas import tpu as pltpu
from jax.sharding import PartitionSpec as P

HEAD_DIM = 128
LEN_MOST = 16


def request_local(lengths_row, tok_count):
    boundary = jnp.cumsum(lengths_row, dtype=jnp.int32)
    position = jnp.arange(tok_count, dtype=jnp.int32)
    return jnp.sum(
        (position[:, None] >= boundary[None, :]).astype(jnp.int32), axis=1, dtype=jnp.int32
    )


def attend_local(queries, key_vals, value_vals, request, head_dim):
    tok_count = queries.shape[0]
    kv_count = key_vals.shape[1] // head_dim
    group_size = queries.shape[1] // key_vals.shape[1]
    query_h = queries.reshape(tok_count, kv_count, group_size, head_dim)
    key_h = key_vals.reshape(tok_count, kv_count, head_dim)
    value_h = value_vals.reshape(tok_count, kv_count, head_dim)
    scores = jnp.einsum(
        "tkgd,skd->kgts", query_h, key_h, preferred_element_type=jnp.float32
    ) * head_dim ** (-0.5)
    position = jnp.arange(tok_count)
    allowed = (request[:, None] == request[None, :]) & (position[None, :] <= position[:, None])
    scores = jnp.where(allowed, scores, -1e30)
    top_score = jnp.max(scores, axis=-1, keepdims=True)
    exp_terms = jnp.exp(scores - top_score)
    softmax_w = (exp_terms / jnp.sum(exp_terms, axis=-1, keepdims=True)).astype(jnp.bfloat16)
    mixed = jnp.einsum("kgts,skd->tkgd", softmax_w, value_h, preferred_element_type=jnp.float32)
    return mixed.astype(jnp.bfloat16).reshape(tok_count, kv_count * group_size * head_dim)


def shards_gathered(
    tokens,
    query_matrix,
    key_matrix,
    value_matrix,
    query_down_maps,
    query_up_maps,
    request_lengths,
    request_adapter,
    adapter_pool_slot,
):
    tok_count = tokens.shape[0]
    feat_count = tokens.shape[1]
    req_count = request_lengths.shape[1]
    adapter_count = adapter_pool_slot.shape[0]
    capacity = max(2, req_count // adapter_count) * LEN_MOST
    request = request_local(request_lengths[0], tok_count)
    slot_table = jnp.sum(
        jnp.where(
            request_adapter[:, 0][:, None] == jnp.arange(adapter_count)[None, :],
            adapter_pool_slot[None, :],
            0,
        ),
        axis=1,
        dtype=jnp.int32,
    )
    row_slot = jnp.sum(
        jnp.where(request[:, None] == jnp.arange(req_count)[None, :], slot_table[None, :], 0),
        axis=1,
        dtype=jnp.int32,
    )
    slot_hit = (row_slot[:, None] == jnp.arange(adapter_count)[None, :]).astype(jnp.int32)
    earlier = jnp.cumsum(slot_hit, axis=0, dtype=jnp.int32) - slot_hit
    target = row_slot * capacity + jnp.sum(earlier * slot_hit, axis=1, dtype=jnp.int32)
    packed = jnp.zeros((adapter_count * capacity, feat_count), jnp.bfloat16).at[target].set(tokens)
    packed = packed.reshape(adapter_count, capacity, feat_count)
    tok_full = lax.all_gather(tokens, "tp", axis=1, tiled=True)
    pieces = (
        lax.all_gather(query_matrix, "pool", axis=0, tiled=True),
        lax.all_gather(key_matrix, "pool", axis=0, tiled=True),
        lax.all_gather(value_matrix, "pool", axis=0, tiled=True),
    )
    query_base, key_raw, value_raw = tuple(
        (
            jnp.dot(tok_full, weight_piece, preferred_element_type=jnp.float32)
            for weight_piece in pieces
        )
    )
    shrunk = jnp.einsum(
        "sjd,sdr->sjr",
        packed,
        lax.all_gather(query_down_maps, "pool", axis=0, tiled=True),
        preferred_element_type=jnp.float32,
    )
    low_rank = lax.psum(shrunk, "tp").astype(jnp.bfloat16)
    delta = jnp.einsum(
        "sjr,srk->sjk",
        low_rank,
        lax.all_gather(query_up_maps, "pool", axis=0, tiled=True),
        preferred_element_type=jnp.float32,
    ).astype(jnp.bfloat16)
    delta_tokens = delta.reshape(adapter_count * capacity, delta.shape[2])[target]
    queries = (query_base + delta_tokens.astype(jnp.float32)).astype(jnp.bfloat16)
    return attend_local(
        queries, key_raw.astype(jnp.bfloat16), value_raw.astype(jnp.bfloat16), request, HEAD_DIM
    )


UNIT = 128


def attend_kernel(group_size, place_ref, own_ref, near_ref, far_ref, delta_ref, bias_ref, *refs):
    out_ref, sum_ref = refs[-2:]
    wide = own_ref[...] + jnp.where(place_ref[3] == 1, near_ref[...], far_ref[...]).astype(jnp.float32)
    sum_ref[:, : 2 * HEAD_DIM] = wide[:, : 2 * HEAD_DIM].astype(jnp.bfloat16)
    sum_ref[:, 2 * HEAD_DIM :] = (wide[:, 2 * HEAD_DIM :] + delta_ref[...].astype(jnp.float32)).astype(jnp.bfloat16)
    for b in range(own_ref.shape[0] // UNIT):
        rows = slice(b * UNIT, (b + 1) * UNIT)
        keys = slice(max(0, b - 1) * UNIT, (b + 1) * UNIT)
        bias = bias_ref[b] if b > 0 else bias_ref[b][:, UNIT:]
        query = jnp.concatenate(
            [sum_ref[rows, (2 + i) * HEAD_DIM : (3 + i) * HEAD_DIM] for i in range(group_size)], axis=0
        )
        scores = lax.dot_general(
            query, sum_ref[keys, :HEAD_DIM], (((1,), (1,)), ((), ())), preferred_element_type=jnp.float32
        ) * HEAD_DIM ** (-0.5)
        scores = scores + jnp.concatenate([bias] * group_size, axis=0)
        exp_terms = jnp.exp(scores - jnp.max(scores, axis=-1, keepdims=True))
        weights = (exp_terms / jnp.sum(exp_terms, axis=-1, keepdims=True)).astype(jnp.bfloat16)
        mixed = jnp.dot(
            weights, sum_ref[keys, HEAD_DIM : 2 * HEAD_DIM], preferred_element_type=jnp.float32
        ).astype(jnp.bfloat16)
        for i in range(group_size):
            out_ref[rows, i * HEAD_DIM : (i + 1) * HEAD_DIM] = mixed[i * UNIT : (i + 1) * UNIT]


def attend_head(kv, kv_count, place, own, near, far, delta, bias, earlier):
    rows, span = own.shape
    group_size = span // HEAD_DIM - 2
    wide = group_size * HEAD_DIM
    whole = [pl.BlockSpec((rows, span), lambda i, b=x.shape[0] // rows - 1: (b, 0)) for x in (own, near, far)]
    specs = [pl.BlockSpec(memory_space=pltpu.SMEM)] + whole + [pl.BlockSpec((rows, wide), lambda i: (0, kv)), pl.BlockSpec(bias.shape, lambda i: (0, 0, 0))]
    operands = [place, own, near, far, delta, bias]
    aliases = {}
    if earlier is not None:
        specs.append(pl.BlockSpec(memory_space=pl.ANY))
        operands.append(earlier)
        aliases = {6: 0}
    return pl.pallas_call(
        functools.partial(attend_kernel, group_size),
        grid=(1,),
        in_specs=specs,
        out_specs=pl.BlockSpec((rows, wide), lambda i: (0, kv)),
        out_shape=jax.ShapeDtypeStruct((rows, kv_count * wide), jnp.bfloat16),
        scratch_shapes=[pltpu.VMEM((rows, span), jnp.bfloat16)],
        input_output_aliases=aliases,
        compiler_params=pltpu.CompilerParams(vmem_limit_bytes=12 * 2**20),
        cost_estimate=pl.CostEstimate(flops=0, bytes_accessed=0, transcendentals=0),
    )(*operands)


def request_bias(request):
    blocks = request.shape[0] // UNIT
    padded = jnp.concatenate([jnp.full((UNIT,), -1, jnp.int32), request])
    keys = jnp.stack([padded[b * UNIT : (b + 2) * UNIT] for b in range(blocks)])
    row = jnp.arange(UNIT)[:, None]
    col = jnp.arange(2 * UNIT)[None, :]
    allowed = (request.reshape(blocks, UNIT, 1) == keys[:, None, :]) & (col <= row + UNIT)[None]
    return jnp.where(allowed, 0.0, -1e30).astype(jnp.float32)


def copy_all(pairs, sems):
    copies = [pltpu.make_async_copy(*pair, sems.at[i]) for i, pair in enumerate(pairs)]
    for copy in copies:
        copy.start()
    for copy in copies:
        copy.wait()


def halves_kernel(tok_ref, top_ref, bottom_ref, sems):
    rows = top_ref.shape[0]
    copy_all([(tok_ref.at[pl.ds(i * rows, rows)], ref) for i, ref in enumerate((top_ref, bottom_ref))], sems)


def cut_kernel(parts, place_ref, key_ref, value_ref, query_ref, *refs):
    pairs = []
    for (kv, sent), out_ref in zip(parts, refs[:-1]):
        count, wide = out_ref.shape[0], out_ref.shape[1] - 2 * HEAD_DIM
        rows = pl.ds(pl.multiple_of(place_ref[2] * count, 64), count) if sent else pl.ds(0, count)
        small = pl.ds(kv * HEAD_DIM, HEAD_DIM)
        pairs.append((key_ref.at[rows, small], out_ref.at[:, pl.ds(0, HEAD_DIM)]))
        pairs.append((value_ref.at[rows, small], out_ref.at[:, pl.ds(HEAD_DIM, HEAD_DIM)]))
        pairs.append((query_ref.at[rows, pl.ds(kv * wide, wide)], out_ref.at[:, pl.ds(2 * HEAD_DIM, wide)]))
    copy_all(pairs, refs[-1])


def copying(kernel, prefetch, operands, outs, copies, grant=60):
    smem = [pl.BlockSpec(memory_space=pltpu.SMEM)] * len(prefetch)
    vmem = pl.BlockSpec(memory_space=pltpu.VMEM)
    return pl.pallas_call(
        kernel,
        in_specs=smem + [pl.BlockSpec(memory_space=pl.ANY)] * len(operands),
        out_specs=[vmem] * len(outs),
        out_shape=outs,
        scratch_shapes=[pltpu.SemaphoreType.DMA((copies,))],
        compiler_params=pltpu.CompilerParams(vmem_limit_bytes=grant * 2**20),
        cost_estimate=pl.CostEstimate(flops=0, bytes_accessed=0, transcendentals=0),
    )(*prefetch, *operands)


def halves(tokens):
    out = jax.ShapeDtypeStruct((tokens.shape[0] // 2, tokens.shape[1]), tokens.dtype)
    return copying(halves_kernel, (), (tokens,), [out, out], 2)


def cut(parts, place, key_matrix, value_matrix, query_matrix):
    feats, narrow = key_matrix.shape
    span = 2 * HEAD_DIM + query_matrix.shape[1] * HEAD_DIM // narrow
    outs = [jax.ShapeDtypeStruct((feats // 2 if sent else feats, span), key_matrix.dtype) for _, sent in parts]
    kernel = functools.partial(cut_kernel, parts)
    grant = 60 if len(parts) == 1 else 24
    return copying(kernel, (place,), (key_matrix, value_matrix, query_matrix), outs, 3 * len(parts), grant)


def sums_kernel(layout, place_ref, *refs):
    weights_ref, theirs_ref, others_ref, out_ref, feats_ref = refs[-5:]
    first_core, group = place_ref[1], place_ref[2]
    share, half = feats_ref.shape[1] // len(layout), theirs_ref.shape[0]
    rest = list(refs[:-5])
    for i, counts in enumerate(layout):
        start = 0 if len(layout) == 1 else (place_ref[0] if i == 0 else 1 - place_ref[0]) * share
        for block, count in zip((1 - first_core, first_core), counts):
            done = 0
            for piece_ref in [rest.pop(0) for _ in range(count)]:
                rows = pl.ds(pl.multiple_of(start + done, 32), piece_ref.shape[0])
                feats_ref[block, rows, :] = piece_ref[...]
                done += piece_ref.shape[0]
    here = pl.ds(pl.multiple_of(group * half, HEAD_DIM), half)
    there = pl.ds(pl.multiple_of((1 - group) * half, HEAD_DIM), half)
    span = out_ref.shape[1]
    step = 2 * HEAD_DIM
    for col in range(0, span, step):
        cols = slice(col, min(span, col + step))
        total = jnp.dot(feats_ref[0], weights_ref[:, cols], preferred_element_type=jnp.float32)
        total += jnp.dot(feats_ref[1, :, here], theirs_ref[:, cols], preferred_element_type=jnp.float32)
        total += jnp.dot(feats_ref[1, :, there], others_ref[:, cols], preferred_element_type=jnp.float32)
        out_ref[:, cols] = total.astype(out_ref.dtype)


def sums(name, place, shares, weights, theirs, others, dtype):
    layout = [tuple(len(pieces) for pieces in share) for share in shares]
    pieces = [x for share in shares for part in share for x in part]
    rows, feats = sum(x.shape[0] for share in shares for x in share[0]), weights.shape[0]
    span = weights.shape[1]
    vmem = pl.BlockSpec(memory_space=pltpu.VMEM)
    with jax.named_scope(name):
        return pl.pallas_call(
            functools.partial(sums_kernel, layout),
            in_specs=[pl.BlockSpec(memory_space=pltpu.SMEM)] + [vmem] * (len(pieces) + 3),
            out_specs=vmem,
            out_shape=jax.ShapeDtypeStruct((rows, span), dtype),
            scratch_shapes=[pltpu.VMEM((2, rows, feats), jnp.bfloat16)],
            compiler_params=pltpu.CompilerParams(vmem_limit_bytes=12 * 2**20),
            cost_estimate=pl.CostEstimate(flops=0, bytes_accessed=0, transcendentals=0),
        )(place, *pieces, weights, theirs, others)


def slot_hits(holder, row_slot, width):
    lane = lax.broadcasted_iota(jnp.int32, (row_slot.shape[0], width), 1)
    return row_slot == holder * 2 + (lane >= width // 2).astype(jnp.int32)


def held_maps(inner, maps, first, buffers, sems):
    rows = buffers.shape[1]
    copy_all([(x.at[pl.ds(first, rows)], buffers.at[i]) for i, x in enumerate(maps)], sems)
    return [buffers[0], buffers[1], buffers[3 - inner], buffers[5 - inner]]


def shrink_kernel(holder_ref, slot_ref, tok_ref, *refs):
    out_ref, buffers, sems = refs[-3:]
    width = buffers.shape[2]
    total = jnp.zeros((tok_ref.shape[0], width), jnp.float32)
    for k, down in enumerate(held_maps(holder_ref[4], refs[:-3], 0, buffers, sems)):
        product = jnp.dot(tok_ref[...], down, preferred_element_type=jnp.float32)
        total += jnp.where(slot_hits(holder_ref[k], slot_ref[...], width), product, 0.0)
    total = total[:, : width // 2] + total[:, width // 2 :]
    half = out_ref.shape[0]
    out_ref[...] = jnp.concatenate([total[:half], total[half:]], axis=1)


def expand_kernel(holder_ref, slot_ref, own_ref, cores_ref, chips_ref, both_ref, *refs):
    out_ref, buffers, sems = refs[-3:]
    width = buffers.shape[2]
    maps = held_maps(holder_ref[4], refs[:-3], refs[0].shape[0] - buffers.shape[1], buffers, sems)
    low_rank = (own_ref[...] + cores_ref[...]) + (chips_ref[...] + both_ref[...])
    low_rank = low_rank.astype(jnp.bfloat16)
    halves = [low_rank[:, : width // 2], low_rank[:, width // 2 :]]
    twice = jnp.concatenate([jnp.concatenate([half, half], axis=1) for half in halves], axis=0)
    total = jnp.zeros(out_ref.shape, jnp.float32)
    for k, up in enumerate(maps):
        spread = jnp.where(slot_hits(holder_ref[k], slot_ref[...], width), twice, jnp.zeros_like(twice))
        total += lax.dot_general(spread, up, (((1,), (1,)), ((), ())), preferred_element_type=jnp.float32)
    out_ref[...] = total.astype(out_ref.dtype)


def adapter_call(name, kernel, shape, rows, holders, operands, maps):
    vmem = pl.BlockSpec(memory_space=pltpu.VMEM)
    with jax.named_scope(name):
        return pl.pallas_call(
            kernel,
            in_specs=[pl.BlockSpec(memory_space=pltpu.SMEM)]
            + [vmem] * len(operands)
            + [pl.BlockSpec(memory_space=pl.ANY)] * len(maps),
            out_specs=vmem,
            out_shape=shape,
            scratch_shapes=[
                pltpu.VMEM((len(maps), rows, maps[0].shape[1]), maps[0].dtype),
                pltpu.SemaphoreType.DMA((len(maps),)),
            ],
            compiler_params=pltpu.CompilerParams(vmem_limit_bytes=12 * 2**20),
            cost_estimate=pl.CostEstimate(flops=0, bytes_accessed=0, transcendentals=0),
        )(holders, *operands, *maps)


PAIRED = (4, 4, 2)
FAR = [(0, 2), (3, 1)]
INNER = [(1, 2), (2, 1), (0, 0), (3, 3)]
OUTWARD = [(1, 0), (2, 3), (0, 1), (3, 2)]


def shards_paired(
    tokens,
    query_matrix,
    key_matrix,
    value_matrix,
    query_down_maps,
    query_up_maps,
    request_lengths,
    request_adapter,
    adapter_pool_slot,
):
    pools, parts, groups = PAIRED
    tok_count, feat_count = tokens.shape
    req_count = request_lengths.shape[1]
    adapter_count = adapter_pool_slot.shape[0]
    slots_own, _, rank = query_down_maps.shape
    group, pool, part = lax.axis_index("groups"), lax.axis_index("pool"), lax.axis_index("tp")
    f32, bf16 = jnp.float32, jnp.bfloat16
    dot = functools.partial(jnp.dot, preferred_element_type=f32)
    here = part // 2 == pool // 2
    first_core = pool % 2 == part % 2
    place = jnp.stack([here.astype(jnp.int32), first_core.astype(jnp.int32), group.astype(jnp.int32), (pool % 3 > 0).astype(jnp.int32)])

    def permute(name, x, axes, pairs):
        with jax.named_scope(name):
            return lax.ppermute(x, axes, pairs)

    def chip_swap(name, x, bits=2):
        return permute(name, x, "tp", [(t, t ^ bits) for t in range(parts)])

    def core_swap(name, x):
        return chip_swap(name, x, 1)

    def after(x, *done):
        return lax.optimization_barrier((x,) + done)[0]

    kv_count = key_matrix.shape[1] // HEAD_DIM
    wide = query_matrix.shape[1] // kv_count
    in_pairs = [(i, i ^ 1) for i in range(pools)]
    replicas = [(g * pools + p, (1 - g) * pools + p) for g in range(groups) for p in range(pools)]
    matrices = key_matrix, value_matrix, query_matrix
    half_rows = tok_count // 2
    (first_send,) = cut([(0, True)], place, *matrices)
    top, bottom = halves(after(tokens, first_send))

    request = request_local(request_lengths[0], tok_count)
    slot_table = jnp.sum(
        jnp.where(
            request_adapter[:, 0][:, None] == jnp.arange(adapter_count)[None, :],
            adapter_pool_slot[None, :],
            0,
        ),
        axis=1,
        dtype=jnp.int32,
    )
    row_slot = jnp.sum(
        jnp.where(request[:, None] == jnp.arange(req_count)[None, :], slot_table[None, :], 0),
        axis=1,
        dtype=jnp.int32,
    )
    bias = request_bias(request)

    top_here = chip_swap("tokens_top", top)
    first = permute("weights_0", first_send, "pool", in_pairs)
    maps = jnp.concatenate(
        [query_down_maps[i] for i in range(slots_own)], axis=1
    ), query_up_maps.reshape(slots_own * rank, -1).T
    maps = after(jnp.concatenate(maps, axis=0), top)
    inner_maps = permute("maps_inner", maps, "pool", INNER)
    leaving = jnp.where(here, after(top_here, maps, row_slot, bias), bottom)
    far = permute("tokens_far", leaving, "pool", FAR)
    later = [(kv, True) for kv in range(1, kv_count)] + [(kv, False) for kv in range(kv_count)]
    send, *weights = cut(later, after(place, leaving), *matrices)
    near = permute("tokens_near", after(leaving, far), "pool", INNER)

    pair_maps = permute("maps_pair", after(maps, first), "pool", in_pairs)
    bottom_here = chip_swap("tokens_bottom", after(bottom, leaving))
    mine = jnp.where(here, tokens, jnp.concatenate([top_here, bottom_here], axis=0))
    own_cores = core_swap("own_cores", mine)
    others = [permute("weights_0_replicas", after(first, send, *weights, inner_maps), ("groups", "pool"), replicas)]
    theirs = [first, permute("weights_1", after(send, pair_maps), "pool", in_pairs)]
    others.append(permute("weights_1_replicas", theirs[1], ("groups", "pool"), replicas))
    far_chips = chip_swap("far_chips", after(far, bottom_here))
    outer_maps = permute("maps_outer", pair_maps, "pool", INNER)
    far_cores = core_swap("far_cores_a", far), core_swap("far_cores_b", after(far_chips, others[0], pair_maps, own_cores))
    far_pieces = [([far], far_cores[:1]), ([far_chips], far_cores[1:])]
    near_chips = chip_swap("near_chips", after(near, far_chips))
    inner_out = permute("maps_inner_out", after(inner_maps, theirs[1]), "pool", OUTWARD)
    outer_out = permute("maps_outer_out", after(outer_maps, theirs[1]), "pool", OUTWARD)
    def part_sums(name, kv, pieces, dtype, earlier=()):
        both = weights[kv], theirs[kv], others[kv]
        return sums(f"{name}_{kv}", after(place, *earlier), pieces, *both, dtype)

    far_0 = part_sums("far", 0, far_pieces, bf16)
    arrived_far = [permute("sums_far_0", far_0, "pool", INNER)]
    near_cores = core_swap("near_cores_a", near)
    fine = half_rows // 2
    near_fine = [core_swap(f"near_cores_b{i}", near_chips[i * fine : (i + 1) * fine]) for i in range(2)]
    near_pieces = [([near], [near_cores]), ([near_chips], near_fine)]
    near_0 = part_sums("near", 0, near_pieces, bf16, (far_0, outer_maps))
    arrived_near = [permute("sums_near_0", after(near_0, arrived_far[0]), "pool", INNER)]
    own_pieces = [([mine], [own_cores])]
    own_0 = part_sums("own", 0, own_pieces, f32, (near_0,))
    far_1 = part_sums("far", 1, far_pieces, bf16, (own_0, inner_out))
    arrived_far.append(permute("sums_far_1", after(far_1, arrived_near[0], arrived_far[0]), "pool", INNER))
    forwarded = [permute("sums_out_0", arrived_far[0], "pool", OUTWARD)]
    own = [own_0, part_sums("own", 1, own_pieces, f32, (far_1,))]

    inner = 2 - pool // 2
    holders = jnp.stack([pool, pool ^ 1, inner, inner ^ 1, place[3]]).astype(jnp.int32)
    held = maps, pair_maps, inner_maps, inner_out, outer_maps, outer_out
    slots = row_slot[:, None]
    shrunk = jax.ShapeDtypeStruct((half_rows, 2 * rank), f32)
    shrunk = adapter_call(
        "low_rank", shrink_kernel, shrunk, feat_count, holders, (slots, after(tokens, near_0)), held
    )
    shares = [shrunk] + [chip_swap(f"low_rank_{bits}", shrunk, bits) for bits in range(1, parts)]
    near_1 = part_sums("near", 1, near_pieces, bf16, (own[1], shrunk))
    arrived_near.append(permute("sums_near_1", after(near_1, arrived_far[1], forwarded[0]), "pool", INNER))
    forwarded.append(permute("sums_out_1", arrived_far[1], "pool", OUTWARD))
    delta = jax.ShapeDtypeStruct((tok_count, query_matrix.shape[1]), bf16)
    delta = adapter_call(
        "delta", expand_kernel, delta, maps.shape[0] - feat_count, holders, (slots, *shares), held
    )
    mixed = None
    for kv in range(kv_count):
        mixed = attend_head(kv, kv_count, place, own[kv], arrived_near[kv], forwarded[kv], delta, bias, mixed)
    return mixed


def solution(mesh):
    placed = (
        P(("groups", "pool"), "tp"),
        P("pool", "tp"),
        P("pool", "tp"),
        P("pool", "tp"),
        P(("groups", "pool"), "tp", None),
        P(("groups", "pool"), None, "tp"),
        P(("groups", "pool"), None),
        P(("groups", "pool"), None),
        P(),
    )
    sizes = mesh.shape
    if (sizes["pool"], sizes["tp"], sizes["groups"]) == PAIRED:
        shards = shards_paired
    else:
        shards = shards_gathered
    return jax.shard_map(
        shards, mesh=mesh, in_specs=placed, out_specs=P(("groups", "pool"), "tp"), check_vma=False
    )
```

```python
import functools

import jax
import jax.numpy as jnp
from jax import lax
from jax.experimental import pallas as pl
from jax.experimental.pallas import tpu as pltpu
from jax.sharding import PartitionSpec as P

HEAD_DIM = 128
LEN_MOST = 16


def request_local(lengths_row, tok_count):
    boundary = jnp.cumsum(lengths_row, dtype=jnp.int32)
    position = jnp.arange(tok_count, dtype=jnp.int32)
    return jnp.sum(
        (position[:, None] >= boundary[None, :]).astype(jnp.int32), axis=1, dtype=jnp.int32
    )


def attend_local(queries, key_vals, value_vals, request, head_dim):
    tok_count = queries.shape[0]
    kv_count = key_vals.shape[1] // head_dim
    group_size = queries.shape[1] // key_vals.shape[1]
    query_h = queries.reshape(tok_count, kv_count, group_size, head_dim)
    key_h = key_vals.reshape(tok_count, kv_count, head_dim)
    value_h = value_vals.reshape(tok_count, kv_count, head_dim)
    scores = jnp.einsum(
        "tkgd,skd->kgts", query_h, key_h, preferred_element_type=jnp.float32
    ) * head_dim ** (-0.5)
    position = jnp.arange(tok_count)
    allowed = (request[:, None] == request[None, :]) & (position[None, :] <= position[:, None])
    scores = jnp.where(allowed, scores, -1e30)
    top_score = jnp.max(scores, axis=-1, keepdims=True)
    exp_terms = jnp.exp(scores - top_score)
    softmax_w = (exp_terms / jnp.sum(exp_terms, axis=-1, keepdims=True)).astype(jnp.bfloat16)
    mixed = jnp.einsum("kgts,skd->tkgd", softmax_w, value_h, preferred_element_type=jnp.float32)
    return mixed.astype(jnp.bfloat16).reshape(tok_count, kv_count * group_size * head_dim)


def shards_gathered(
    tokens,
    query_matrix,
    key_matrix,
    value_matrix,
    query_down_maps,
    query_up_maps,
    request_lengths,
    request_adapter,
    adapter_pool_slot,
):
    tok_count = tokens.shape[0]
    feat_count = tokens.shape[1]
    req_count = request_lengths.shape[1]
    adapter_count = adapter_pool_slot.shape[0]
    capacity = max(2, req_count // adapter_count) * LEN_MOST
    request = request_local(request_lengths[0], tok_count)
    slot_table = jnp.sum(
        jnp.where(
            request_adapter[:, 0][:, None] == jnp.arange(adapter_count)[None, :],
            adapter_pool_slot[None, :],
            0,
        ),
        axis=1,
        dtype=jnp.int32,
    )
    row_slot = jnp.sum(
        jnp.where(request[:, None] == jnp.arange(req_count)[None, :], slot_table[None, :], 0),
        axis=1,
        dtype=jnp.int32,
    )
    slot_hit = (row_slot[:, None] == jnp.arange(adapter_count)[None, :]).astype(jnp.int32)
    earlier = jnp.cumsum(slot_hit, axis=0, dtype=jnp.int32) - slot_hit
    target = row_slot * capacity + jnp.sum(earlier * slot_hit, axis=1, dtype=jnp.int32)
    packed = jnp.zeros((adapter_count * capacity, feat_count), jnp.bfloat16).at[target].set(tokens)
    packed = packed.reshape(adapter_count, capacity, feat_count)
    tok_full = lax.all_gather(tokens, "tp", axis=1, tiled=True)
    pieces = (
        lax.all_gather(query_matrix, "pool", axis=0, tiled=True),
        lax.all_gather(key_matrix, "pool", axis=0, tiled=True),
        lax.all_gather(value_matrix, "pool", axis=0, tiled=True),
    )
    query_base, key_raw, value_raw = tuple(
        (
            jnp.dot(tok_full, weight_piece, preferred_element_type=jnp.float32)
            for weight_piece in pieces
        )
    )
    shrunk = jnp.einsum(
        "sjd,sdr->sjr",
        packed,
        lax.all_gather(query_down_maps, "pool", axis=0, tiled=True),
        preferred_element_type=jnp.float32,
    )
    low_rank = lax.psum(shrunk, "tp").astype(jnp.bfloat16)
    delta = jnp.einsum(
        "sjr,srk->sjk",
        low_rank,
        lax.all_gather(query_up_maps, "pool", axis=0, tiled=True),
        preferred_element_type=jnp.float32,
    ).astype(jnp.bfloat16)
    delta_tokens = delta.reshape(adapter_count * capacity, delta.shape[2])[target]
    queries = (query_base + delta_tokens.astype(jnp.float32)).astype(jnp.bfloat16)
    return attend_local(
        queries, key_raw.astype(jnp.bfloat16), value_raw.astype(jnp.bfloat16), request, HEAD_DIM
    )


UNIT = 128


def attend_kernel(group_size, place_ref, own_ref, near_ref, far_ref, delta_ref, bias_ref, *refs):
    out_ref, sum_ref = refs[-2:]
    wide = own_ref[...] + jnp.where(place_ref[3] == 1, near_ref[...], far_ref[...]).astype(jnp.float32)
    sum_ref[:, : 2 * HEAD_DIM] = wide[:, : 2 * HEAD_DIM].astype(jnp.bfloat16)
    sum_ref[:, 2 * HEAD_DIM :] = (wide[:, 2 * HEAD_DIM :] + delta_ref[...].astype(jnp.float32)).astype(jnp.bfloat16)
    for b in range(own_ref.shape[0] // UNIT):
        rows = slice(b * UNIT, (b + 1) * UNIT)
        keys = slice(max(0, b - 1) * UNIT, (b + 1) * UNIT)
        bias = bias_ref[b] if b > 0 else bias_ref[b][:, UNIT:]
        query = jnp.concatenate(
            [sum_ref[rows, (2 + i) * HEAD_DIM : (3 + i) * HEAD_DIM] for i in range(group_size)], axis=0
        )
        scores = lax.dot_general(
            query, sum_ref[keys, :HEAD_DIM], (((1,), (1,)), ((), ())), preferred_element_type=jnp.float32
        ) * HEAD_DIM ** (-0.5)
        scores = scores + jnp.concatenate([bias] * group_size, axis=0)
        exp_terms = jnp.exp(scores - jnp.max(scores, axis=-1, keepdims=True))
        weights = (exp_terms / jnp.sum(exp_terms, axis=-1, keepdims=True)).astype(jnp.bfloat16)
        mixed = jnp.dot(
            weights, sum_ref[keys, HEAD_DIM : 2 * HEAD_DIM], preferred_element_type=jnp.float32
        ).astype(jnp.bfloat16)
        for i in range(group_size):
            out_ref[rows, i * HEAD_DIM : (i + 1) * HEAD_DIM] = mixed[i * UNIT : (i + 1) * UNIT]


def attend_head(kv, kv_count, place, own, near, far, delta, bias, earlier):
    rows, span = own.shape
    group_size = span // HEAD_DIM - 2
    wide = group_size * HEAD_DIM
    whole = [pl.BlockSpec((rows, span), lambda i, b=x.shape[0] // rows - 1: (b, 0)) for x in (own, near, far)]
    specs = [pl.BlockSpec(memory_space=pltpu.SMEM)] + whole + [pl.BlockSpec((rows, wide), lambda i: (0, kv)), pl.BlockSpec(bias.shape, lambda i: (0, 0, 0))]
    operands = [place, own, near, far, delta, bias]
    aliases = {}
    if earlier is not None:
        specs.append(pl.BlockSpec(memory_space=pl.ANY))
        operands.append(earlier)
        aliases = {6: 0}
    return pl.pallas_call(
        functools.partial(attend_kernel, group_size),
        grid=(1,),
        in_specs=specs,
        out_specs=pl.BlockSpec((rows, wide), lambda i: (0, kv)),
        out_shape=jax.ShapeDtypeStruct((rows, kv_count * wide), jnp.bfloat16),
        scratch_shapes=[pltpu.VMEM((rows, span), jnp.bfloat16)],
        input_output_aliases=aliases,
        compiler_params=pltpu.CompilerParams(vmem_limit_bytes=12 * 2**20),
        cost_estimate=pl.CostEstimate(flops=0, bytes_accessed=0, transcendentals=0),
    )(*operands)


def request_bias(request):
    blocks = request.shape[0] // UNIT
    padded = jnp.concatenate([jnp.full((UNIT,), -1, jnp.int32), request])
    keys = jnp.stack([padded[b * UNIT : (b + 2) * UNIT] for b in range(blocks)])
    row = jnp.arange(UNIT)[:, None]
    col = jnp.arange(2 * UNIT)[None, :]
    allowed = (request.reshape(blocks, UNIT, 1) == keys[:, None, :]) & (col <= row + UNIT)[None]
    return jnp.where(allowed, 0.0, -1e30).astype(jnp.float32)


def copy_all(pairs, sems):
    copies = [pltpu.make_async_copy(*pair, sems.at[i]) for i, pair in enumerate(pairs)]
    for copy in copies:
        copy.start()
    for copy in copies:
        copy.wait()


def halves_kernel(tok_ref, top_ref, bottom_ref, sems):
    rows = top_ref.shape[0]
    copy_all([(tok_ref.at[pl.ds(i * rows, rows)], ref) for i, ref in enumerate((top_ref, bottom_ref))], sems)


def cut_kernel(parts, place_ref, key_ref, value_ref, query_ref, *refs):
    pairs = []
    for (kv, sent), out_ref in zip(parts, refs[:-1]):
        count, wide = out_ref.shape[0], out_ref.shape[1] - 2 * HEAD_DIM
        rows = pl.ds(pl.multiple_of(place_ref[2] * count, 64), count) if sent else pl.ds(0, count)
        small = pl.ds(kv * HEAD_DIM, HEAD_DIM)
        pairs.append((key_ref.at[rows, small], out_ref.at[:, pl.ds(0, HEAD_DIM)]))
        pairs.append((value_ref.at[rows, small], out_ref.at[:, pl.ds(HEAD_DIM, HEAD_DIM)]))
        pairs.append((query_ref.at[rows, pl.ds(kv * wide, wide)], out_ref.at[:, pl.ds(2 * HEAD_DIM, wide)]))
    copy_all(pairs, refs[-1])


def copying(kernel, prefetch, operands, outs, copies, grant=60):
    smem = [pl.BlockSpec(memory_space=pltpu.SMEM)] * len(prefetch)
    vmem = pl.BlockSpec(memory_space=pltpu.VMEM)
    return pl.pallas_call(
        kernel,
        in_specs=smem + [pl.BlockSpec(memory_space=pl.ANY)] * len(operands),
        out_specs=[vmem] * len(outs),
        out_shape=outs,
        scratch_shapes=[pltpu.SemaphoreType.DMA((copies,))],
        compiler_params=pltpu.CompilerParams(vmem_limit_bytes=grant * 2**20),
        cost_estimate=pl.CostEstimate(flops=0, bytes_accessed=0, transcendentals=0),
    )(*prefetch, *operands)


def halves(tokens):
    out = jax.ShapeDtypeStruct((tokens.shape[0] // 2, tokens.shape[1]), tokens.dtype)
    return copying(halves_kernel, (), (tokens,), [out, out], 2)


def cut(parts, place, key_matrix, value_matrix, query_matrix):
    feats, narrow = key_matrix.shape
    span = 2 * HEAD_DIM + query_matrix.shape[1] * HEAD_DIM // narrow
    outs = [jax.ShapeDtypeStruct((feats // 2 if sent else feats, span), key_matrix.dtype) for _, sent in parts]
    kernel = functools.partial(cut_kernel, parts)
    grant = 60 if len(parts) == 1 else 24
    return copying(kernel, (place,), (key_matrix, value_matrix, query_matrix), outs, 3 * len(parts), grant)


def sums_kernel(layout, begun, place_ref, *refs):
    if begun:
        weights_ref, theirs_ref, out_ref, rows_ref, feats_ref = refs[-5:]
        begun_refs = out_ref, rows_ref
    else:
        weights_ref, theirs_ref, others_ref, out_ref, feats_ref = refs[-5:]
        begun_refs = ()
    first_core, group = place_ref[1], place_ref[2]
    share, half = feats_ref.shape[1] // len(layout), theirs_ref.shape[0]
    rest = list(refs[:-5])
    for i, counts in enumerate(layout):
        start = 0 if len(layout) == 1 else (place_ref[0] if i == 0 else 1 - place_ref[0]) * share
        for block, count in zip((1 - first_core, first_core), counts):
            done = 0
            for piece_ref in [rest.pop(0) for _ in range(count)]:
                rows = pl.ds(pl.multiple_of(start + done, 32), piece_ref.shape[0])
                feats_ref[block, rows, :] = piece_ref[...]
                done += piece_ref.shape[0]
    here = pl.ds(pl.multiple_of(group * half, HEAD_DIM), half)
    there = pl.ds(pl.multiple_of((1 - group) * half, HEAD_DIM), half)
    span = out_ref.shape[1]
    step = 2 * HEAD_DIM
    if begun_refs:
        begun_refs[1][...] = feats_ref[1, :, there]
    for col in range(0, span, step):
        cols = slice(col, min(span, col + step))
        total = jnp.dot(feats_ref[0], weights_ref[:, cols], preferred_element_type=jnp.float32)
        total += jnp.dot(feats_ref[1, :, here], theirs_ref[:, cols], preferred_element_type=jnp.float32)
        if not begun_refs:
            total += jnp.dot(feats_ref[1, :, there], others_ref[:, cols], preferred_element_type=jnp.float32)
        out_ref[:, cols] = total.astype(out_ref.dtype)


def finish_kernel(begun_ref, feats_ref, others_ref, out_ref):
    total = jnp.dot(feats_ref[...], others_ref[...], preferred_element_type=jnp.float32)
    out_ref[...] = (begun_ref[...] + total).astype(out_ref.dtype)


def finish(name, begun, others, dtype):
    vmem = pl.BlockSpec(memory_space=pltpu.VMEM)
    with jax.named_scope(name):
        return pl.pallas_call(
            finish_kernel,
            in_specs=[vmem] * 3,
            out_specs=vmem,
            out_shape=jax.ShapeDtypeStruct(begun[0].shape, dtype),
            compiler_params=pltpu.CompilerParams(vmem_limit_bytes=12 * 2**20),
            cost_estimate=pl.CostEstimate(flops=0, bytes_accessed=0, transcendentals=0),
        )(*begun, others)


def sums(name, place, shares, weights, theirs, others, dtype):
    layout = [tuple(len(pieces) for pieces in share) for share in shares]
    pieces = [x for share in shares for part in share for x in part]
    rows, feats = sum(x.shape[0] for share in shares for x in share[0]), weights.shape[0]
    span, half = weights.shape[1], theirs.shape[0]
    operands = [*pieces, weights, theirs] + ([] if others is None else [others])
    vmem = pl.BlockSpec(memory_space=pltpu.VMEM)
    out = jax.ShapeDtypeStruct((rows, span), dtype)
    if others is None:
        out = [out, jax.ShapeDtypeStruct((rows, half), weights.dtype)]
    with jax.named_scope(name):
        return pl.pallas_call(
            functools.partial(sums_kernel, layout, others is None),
            in_specs=[pl.BlockSpec(memory_space=pltpu.SMEM)] + [vmem] * len(operands),
            out_specs=vmem if others is not None else [vmem] * 2,
            out_shape=out,
            scratch_shapes=[pltpu.VMEM((2, rows, feats), jnp.bfloat16)],
            compiler_params=pltpu.CompilerParams(vmem_limit_bytes=12 * 2**20),
            cost_estimate=pl.CostEstimate(flops=0, bytes_accessed=0, transcendentals=0),
        )(place, *operands)


def slot_hits(holder, row_slot, width):
    lane = lax.broadcasted_iota(jnp.int32, (row_slot.shape[0], width), 1)
    return row_slot == holder * 2 + (lane >= width // 2).astype(jnp.int32)


def held_maps(inner, maps, first, buffers, sems):
    rows = buffers.shape[1]
    copy_all([(x.at[pl.ds(first, rows)], buffers.at[i]) for i, x in enumerate(maps)], sems)
    return [buffers[0], buffers[1], buffers[3 - inner], buffers[5 - inner]]


def shrink_kernel(holder_ref, slot_ref, tok_ref, *refs):
    out_ref, buffers, sems = refs[-3:]
    width = buffers.shape[2]
    total = jnp.zeros((tok_ref.shape[0], width), jnp.float32)
    for k, down in enumerate(held_maps(holder_ref[4], refs[:-3], 0, buffers, sems)):
        product = jnp.dot(tok_ref[...], down, preferred_element_type=jnp.float32)
        total += jnp.where(slot_hits(holder_ref[k], slot_ref[...], width), product, 0.0)
    total = total[:, : width // 2] + total[:, width // 2 :]
    half = out_ref.shape[0]
    out_ref[...] = jnp.concatenate([total[:half], total[half:]], axis=1)


def expand_kernel(holder_ref, slot_ref, own_ref, cores_ref, chips_ref, both_ref, *refs):
    out_ref, buffers, sems = refs[-3:]
    width = buffers.shape[2]
    maps = held_maps(holder_ref[4], refs[:-3], refs[0].shape[0] - buffers.shape[1], buffers, sems)
    low_rank = (own_ref[...] + cores_ref[...]) + (chips_ref[...] + both_ref[...])
    low_rank = low_rank.astype(jnp.bfloat16)
    halves = [low_rank[:, : width // 2], low_rank[:, width // 2 :]]
    twice = jnp.concatenate([jnp.concatenate([half, half], axis=1) for half in halves], axis=0)
    total = jnp.zeros(out_ref.shape, jnp.float32)
    for k, up in enumerate(maps):
        spread = jnp.where(slot_hits(holder_ref[k], slot_ref[...], width), twice, jnp.zeros_like(twice))
        total += lax.dot_general(spread, up, (((1,), (1,)), ((), ())), preferred_element_type=jnp.float32)
    out_ref[...] = total.astype(out_ref.dtype)


def adapter_call(name, kernel, shape, rows, holders, operands, maps):
    vmem = pl.BlockSpec(memory_space=pltpu.VMEM)
    with jax.named_scope(name):
        return pl.pallas_call(
            kernel,
            in_specs=[pl.BlockSpec(memory_space=pltpu.SMEM)]
            + [vmem] * len(operands)
            + [pl.BlockSpec(memory_space=pl.ANY)] * len(maps),
            out_specs=vmem,
            out_shape=shape,
            scratch_shapes=[
                pltpu.VMEM((len(maps), rows, maps[0].shape[1]), maps[0].dtype),
                pltpu.SemaphoreType.DMA((len(maps),)),
            ],
            compiler_params=pltpu.CompilerParams(vmem_limit_bytes=12 * 2**20),
            cost_estimate=pl.CostEstimate(flops=0, bytes_accessed=0, transcendentals=0),
        )(holders, *operands, *maps)


PAIRED = (4, 4, 2)
FAR = [(0, 2), (3, 1)]
INNER = [(1, 2), (2, 1), (0, 0), (3, 3)]
OUTWARD = [(1, 0), (2, 3), (0, 1), (3, 2)]


def shards_paired(
    tokens,
    query_matrix,
    key_matrix,
    value_matrix,
    query_down_maps,
    query_up_maps,
    request_lengths,
    request_adapter,
    adapter_pool_slot,
):
    pools, parts, groups = PAIRED
    tok_count, feat_count = tokens.shape
    req_count = request_lengths.shape[1]
    adapter_count = adapter_pool_slot.shape[0]
    slots_own, _, rank = query_down_maps.shape
    group, pool, part = lax.axis_index("groups"), lax.axis_index("pool"), lax.axis_index("tp")
    f32, bf16 = jnp.float32, jnp.bfloat16
    dot = functools.partial(jnp.dot, preferred_element_type=f32)
    here = part // 2 == pool // 2
    first_core = pool % 2 == part % 2
    place = jnp.stack([here.astype(jnp.int32), first_core.astype(jnp.int32), group.astype(jnp.int32), (pool % 3 > 0).astype(jnp.int32)])

    def permute(name, x, axes, pairs):
        with jax.named_scope(name):
            return lax.ppermute(x, axes, pairs)

    def chip_swap(name, x, bits=2):
        return permute(name, x, "tp", [(t, t ^ bits) for t in range(parts)])

    def core_swap(name, x):
        return chip_swap(name, x, 1)

    def after(x, *done):
        return lax.optimization_barrier((x,) + done)[0]

    kv_count = key_matrix.shape[1] // HEAD_DIM
    wide = query_matrix.shape[1] // kv_count
    in_pairs = [(i, i ^ 1) for i in range(pools)]
    replicas = [(g * pools + p, (1 - g) * pools + p) for g in range(groups) for p in range(pools)]
    matrices = key_matrix, value_matrix, query_matrix
    half_rows = tok_count // 2
    (first_send,) = cut([(0, True)], place, *matrices)
    top, bottom = halves(after(tokens, first_send))

    request = request_local(request_lengths[0], tok_count)
    slot_table = jnp.sum(
        jnp.where(
            request_adapter[:, 0][:, None] == jnp.arange(adapter_count)[None, :],
            adapter_pool_slot[None, :],
            0,
        ),
        axis=1,
        dtype=jnp.int32,
    )
    row_slot = jnp.sum(
        jnp.where(request[:, None] == jnp.arange(req_count)[None, :], slot_table[None, :], 0),
        axis=1,
        dtype=jnp.int32,
    )
    bias = request_bias(request)

    top_here = chip_swap("tokens_top", top)
    first = permute("weights_0", first_send, "pool", in_pairs)
    maps = jnp.concatenate(
        [query_down_maps[i] for i in range(slots_own)], axis=1
    ), query_up_maps.reshape(slots_own * rank, -1).T
    maps = after(jnp.concatenate(maps, axis=0), top)
    inner_maps = permute("maps_inner", maps, "pool", INNER)
    leaving = jnp.where(here, after(top_here, maps, row_slot, bias), bottom)
    far = permute("tokens_far", leaving, "pool", FAR)
    later = [(kv, True) for kv in range(1, kv_count)] + [(kv, False) for kv in range(kv_count)]
    send, *weights = cut(later, after(place, leaving), *matrices)
    near = permute("tokens_near", after(leaving, far), "pool", INNER)

    pair_maps = permute("maps_pair", after(maps, first), "pool", in_pairs)
    bottom_here = chip_swap("tokens_bottom", after(bottom, leaving))
    mine = jnp.where(here, tokens, jnp.concatenate([top_here, bottom_here], axis=0))
    own_cores = core_swap("own_cores", mine)
    others = [permute("weights_0_replicas", after(first, send, *weights, inner_maps), ("groups", "pool"), replicas)]
    theirs = [first, permute("weights_1", after(send, pair_maps), "pool", in_pairs)]
    others.append(permute("weights_1_replicas", theirs[1], ("groups", "pool"), replicas))
    far_chips = chip_swap("far_chips", after(far, bottom_here))
    outer_maps = permute("maps_outer", pair_maps, "pool", INNER)
    far_cores = core_swap("far_cores_a", far), core_swap("far_cores_b", after(far_chips, others[0], pair_maps, own_cores))
    far_pieces = [([far], far_cores[:1]), ([far_chips], far_cores[1:])]
    near_chips = chip_swap("near_chips", after(near, far_chips))
    inner_out = permute("maps_inner_out", after(inner_maps, theirs[1]), "pool", OUTWARD)
    outer_out = permute("maps_outer_out", after(outer_maps, theirs[1]), "pool", OUTWARD)
    def part_sums(name, kv, pieces, dtype, earlier=()):
        both = weights[kv], theirs[kv], others[kv]
        return sums(f"{name}_{kv}", after(place, *earlier), pieces, *both, dtype)

    far_0 = part_sums("far", 0, far_pieces, bf16)
    arrived_far = [permute("sums_far_0", far_0, "pool", INNER)]
    near_cores = core_swap("near_cores_a", near)
    fine = half_rows // 2
    near_fine = [core_swap(f"near_cores_b{i}", near_chips[i * fine : (i + 1) * fine]) for i in range(2)]
    near_pieces = [([near], [near_cores]), ([near_chips], near_fine)]
    near_0 = part_sums("near", 0, near_pieces, bf16, (far_0, outer_maps))
    arrived_near = [permute("sums_near_0", after(near_0, arrived_far[0]), "pool", INNER)]
    own_pieces = [([mine], [own_cores])]
    own_0 = part_sums("own", 0, own_pieces, f32, (near_0,))
    begun = sums("far_1_begun", after(place, near_0), far_pieces, weights[1], theirs[1], None, f32)
    far_1 = finish("far_1", begun, after(others[1], own_0, inner_out), bf16)
    arrived_far.append(permute("sums_far_1", after(far_1, arrived_near[0], arrived_far[0]), "pool", INNER))
    forwarded = [permute("sums_out_0", arrived_far[0], "pool", OUTWARD)]
    own = [own_0, part_sums("own", 1, own_pieces, f32, (far_1,))]

    inner = 2 - pool // 2
    holders = jnp.stack([pool, pool ^ 1, inner, inner ^ 1, place[3]]).astype(jnp.int32)
    held = maps, pair_maps, inner_maps, inner_out, outer_maps, outer_out
    slots = row_slot[:, None]
    shrunk = jax.ShapeDtypeStruct((half_rows, 2 * rank), f32)
    shrunk = adapter_call(
        "low_rank", shrink_kernel, shrunk, feat_count, holders, (slots, after(tokens, near_0)), held
    )
    shares = [shrunk] + [chip_swap(f"low_rank_{bits}", shrunk, bits) for bits in range(1, parts)]
    near_1 = part_sums("near", 1, near_pieces, bf16, (shrunk,))
    arrived_near.append(permute("sums_near_1", after(near_1, arrived_far[1]), "pool", INNER))
    forwarded.append(permute("sums_out_1", arrived_far[1], "pool", OUTWARD))
    delta = jax.ShapeDtypeStruct((tok_count, query_matrix.shape[1]), bf16)
    delta = adapter_call(
        "delta", expand_kernel, delta, maps.shape[0] - feat_count, after(holders, own[1], forwarded[0]), (slots, *shares), held
    )
    mixed = None
    for kv in range(kv_count):
        mixed = attend_head(kv, kv_count, place, own[kv], arrived_near[kv], forwarded[kv], delta, bias, mixed)
    return mixed


def solution(mesh):
    placed = (
        P(("groups", "pool"), "tp"),
        P("pool", "tp"),
        P("pool", "tp"),
        P("pool", "tp"),
        P(("groups", "pool"), "tp", None),
        P(("groups", "pool"), None, "tp"),
        P(("groups", "pool"), None),
        P(("groups", "pool"), None),
        P(),
    )
    sizes = mesh.shape
    if (sizes["pool"], sizes["tp"], sizes["groups"]) == PAIRED:
        shards = shards_paired
    else:
        shards = shards_gathered
    return jax.shard_map(
        shards, mesh=mesh, in_specs=placed, out_specs=P(("groups", "pool"), "tp"), check_vma=False
    )
```

```python
import functools

import jax
import jax.numpy as jnp
from jax import lax
from jax.experimental import pallas as pl
from jax.experimental.pallas import tpu as pltpu
from jax.sharding import PartitionSpec as P

HEAD_DIM = 128
LEN_MOST = 16


def request_local(lengths_row, tok_count):
    boundary = jnp.cumsum(lengths_row, dtype=jnp.int32)
    position = jnp.arange(tok_count, dtype=jnp.int32)
    return jnp.sum(
        (position[:, None] >= boundary[None, :]).astype(jnp.int32), axis=1, dtype=jnp.int32
    )


def attend_local(queries, key_vals, value_vals, request, head_dim):
    tok_count = queries.shape[0]
    kv_count = key_vals.shape[1] // head_dim
    group_size = queries.shape[1] // key_vals.shape[1]
    query_h = queries.reshape(tok_count, kv_count, group_size, head_dim)
    key_h = key_vals.reshape(tok_count, kv_count, head_dim)
    value_h = value_vals.reshape(tok_count, kv_count, head_dim)
    scores = jnp.einsum(
        "tkgd,skd->kgts", query_h, key_h, preferred_element_type=jnp.float32
    ) * head_dim ** (-0.5)
    position = jnp.arange(tok_count)
    allowed = (request[:, None] == request[None, :]) & (position[None, :] <= position[:, None])
    scores = jnp.where(allowed, scores, -1e30)
    top_score = jnp.max(scores, axis=-1, keepdims=True)
    exp_terms = jnp.exp(scores - top_score)
    softmax_w = (exp_terms / jnp.sum(exp_terms, axis=-1, keepdims=True)).astype(jnp.bfloat16)
    mixed = jnp.einsum("kgts,skd->tkgd", softmax_w, value_h, preferred_element_type=jnp.float32)
    return mixed.astype(jnp.bfloat16).reshape(tok_count, kv_count * group_size * head_dim)


def shards_gathered(
    tokens,
    query_matrix,
    key_matrix,
    value_matrix,
    query_down_maps,
    query_up_maps,
    request_lengths,
    request_adapter,
    adapter_pool_slot,
):
    tok_count = tokens.shape[0]
    feat_count = tokens.shape[1]
    req_count = request_lengths.shape[1]
    adapter_count = adapter_pool_slot.shape[0]
    capacity = max(2, req_count // adapter_count) * LEN_MOST
    request = request_local(request_lengths[0], tok_count)
    slot_table = jnp.sum(
        jnp.where(
            request_adapter[:, 0][:, None] == jnp.arange(adapter_count)[None, :],
            adapter_pool_slot[None, :],
            0,
        ),
        axis=1,
        dtype=jnp.int32,
    )
    row_slot = jnp.sum(
        jnp.where(request[:, None] == jnp.arange(req_count)[None, :], slot_table[None, :], 0),
        axis=1,
        dtype=jnp.int32,
    )
    slot_hit = (row_slot[:, None] == jnp.arange(adapter_count)[None, :]).astype(jnp.int32)
    earlier = jnp.cumsum(slot_hit, axis=0, dtype=jnp.int32) - slot_hit
    target = row_slot * capacity + jnp.sum(earlier * slot_hit, axis=1, dtype=jnp.int32)
    packed = jnp.zeros((adapter_count * capacity, feat_count), jnp.bfloat16).at[target].set(tokens)
    packed = packed.reshape(adapter_count, capacity, feat_count)
    tok_full = lax.all_gather(tokens, "tp", axis=1, tiled=True)
    pieces = (
        lax.all_gather(query_matrix, "pool", axis=0, tiled=True),
        lax.all_gather(key_matrix, "pool", axis=0, tiled=True),
        lax.all_gather(value_matrix, "pool", axis=0, tiled=True),
    )
    query_base, key_raw, value_raw = tuple(
        (
            jnp.dot(tok_full, weight_piece, preferred_element_type=jnp.float32)
            for weight_piece in pieces
        )
    )
    shrunk = jnp.einsum(
        "sjd,sdr->sjr",
        packed,
        lax.all_gather(query_down_maps, "pool", axis=0, tiled=True),
        preferred_element_type=jnp.float32,
    )
    low_rank = lax.psum(shrunk, "tp").astype(jnp.bfloat16)
    delta = jnp.einsum(
        "sjr,srk->sjk",
        low_rank,
        lax.all_gather(query_up_maps, "pool", axis=0, tiled=True),
        preferred_element_type=jnp.float32,
    ).astype(jnp.bfloat16)
    delta_tokens = delta.reshape(adapter_count * capacity, delta.shape[2])[target]
    queries = (query_base + delta_tokens.astype(jnp.float32)).astype(jnp.bfloat16)
    return attend_local(
        queries, key_raw.astype(jnp.bfloat16), value_raw.astype(jnp.bfloat16), request, HEAD_DIM
    )


UNIT = 128


def attend_kernel(group_size, place_ref, own_ref, near_ref, far_ref, delta_ref, bias_ref, *refs):
    out_ref, sum_ref = refs[-2:]
    wide = own_ref[...] + jnp.where(place_ref[3] == 1, near_ref[...], far_ref[...]).astype(jnp.float32)
    sum_ref[:, : 2 * HEAD_DIM] = wide[:, : 2 * HEAD_DIM].astype(jnp.bfloat16)
    sum_ref[:, 2 * HEAD_DIM :] = (wide[:, 2 * HEAD_DIM :] + delta_ref[...].astype(jnp.float32)).astype(jnp.bfloat16)
    for b in range(own_ref.shape[0] // UNIT):
        rows = slice(b * UNIT, (b + 1) * UNIT)
        keys = slice(max(0, b - 1) * UNIT, (b + 1) * UNIT)
        bias = bias_ref[b] if b > 0 else bias_ref[b][:, UNIT:]
        query = jnp.concatenate(
            [sum_ref[rows, (2 + i) * HEAD_DIM : (3 + i) * HEAD_DIM] for i in range(group_size)], axis=0
        )
        scores = lax.dot_general(
            query, sum_ref[keys, :HEAD_DIM], (((1,), (1,)), ((), ())), preferred_element_type=jnp.float32
        ) * HEAD_DIM ** (-0.5)
        scores = scores + jnp.concatenate([bias] * group_size, axis=0)
        exp_terms = jnp.exp(scores - jnp.max(scores, axis=-1, keepdims=True))
        weights = (exp_terms * (1.0 / jnp.sum(exp_terms, axis=-1, keepdims=True))).astype(jnp.bfloat16)
        mixed = jnp.dot(
            weights, sum_ref[keys, HEAD_DIM : 2 * HEAD_DIM], preferred_element_type=jnp.float32
        ).astype(jnp.bfloat16)
        for i in range(group_size):
            out_ref[rows, i * HEAD_DIM : (i + 1) * HEAD_DIM] = mixed[i * UNIT : (i + 1) * UNIT]


def attend_head(kv, kv_count, place, own, near, far, delta, bias, earlier):
    rows, span = own.shape
    group_size = span // HEAD_DIM - 2
    wide = group_size * HEAD_DIM
    whole = [pl.BlockSpec((rows, span), lambda i, b=x.shape[0] // rows - 1: (b, 0)) for x in (own, near, far)]
    specs = [pl.BlockSpec(memory_space=pltpu.SMEM)] + whole + [pl.BlockSpec((rows, wide), lambda i: (0, kv)), pl.BlockSpec(bias.shape, lambda i: (0, 0, 0))]
    operands = [place, own, near, far, delta, bias]
    aliases = {}
    if earlier is not None:
        specs.append(pl.BlockSpec(memory_space=pl.ANY))
        operands.append(earlier)
        aliases = {6: 0}
    return pl.pallas_call(
        functools.partial(attend_kernel, group_size),
        grid=(1,),
        in_specs=specs,
        out_specs=pl.BlockSpec((rows, wide), lambda i: (0, kv)),
        out_shape=jax.ShapeDtypeStruct((rows, kv_count * wide), jnp.bfloat16),
        scratch_shapes=[pltpu.VMEM((rows, span), jnp.bfloat16)],
        input_output_aliases=aliases,
        compiler_params=pltpu.CompilerParams(vmem_limit_bytes=12 * 2**20),
        cost_estimate=pl.CostEstimate(flops=0, bytes_accessed=0, transcendentals=0),
    )(*operands)


def request_bias(request):
    blocks = request.shape[0] // UNIT
    padded = jnp.concatenate([jnp.full((UNIT,), -1, jnp.int32), request])
    keys = jnp.stack([padded[b * UNIT : (b + 2) * UNIT] for b in range(blocks)])
    row = jnp.arange(UNIT)[:, None]
    col = jnp.arange(2 * UNIT)[None, :]
    allowed = (request.reshape(blocks, UNIT, 1) == keys[:, None, :]) & (col <= row + UNIT)[None]
    return jnp.where(allowed, 0.0, -1e30).astype(jnp.float32)


def copy_all(pairs, sems):
    copies = [pltpu.make_async_copy(*pair, sems.at[i]) for i, pair in enumerate(pairs)]
    for copy in copies:
        copy.start()
    for copy in copies:
        copy.wait()


def halves_kernel(tok_ref, top_ref, bottom_ref, sems):
    rows = top_ref.shape[0]
    copy_all([(tok_ref.at[pl.ds(i * rows, rows)], ref) for i, ref in enumerate((top_ref, bottom_ref))], sems)


def cut_kernel(parts, place_ref, key_ref, value_ref, query_ref, *refs):
    pairs = []
    for (kv, sent), out_ref in zip(parts, refs[:-1]):
        count, wide = out_ref.shape[0], out_ref.shape[1] - 2 * HEAD_DIM
        rows = pl.ds(pl.multiple_of(place_ref[2] * count, 64), count) if sent else pl.ds(0, count)
        small = pl.ds(kv * HEAD_DIM, HEAD_DIM)
        pairs.append((key_ref.at[rows, small], out_ref.at[:, pl.ds(0, HEAD_DIM)]))
        pairs.append((value_ref.at[rows, small], out_ref.at[:, pl.ds(HEAD_DIM, HEAD_DIM)]))
        pairs.append((query_ref.at[rows, pl.ds(kv * wide, wide)], out_ref.at[:, pl.ds(2 * HEAD_DIM, wide)]))
    copy_all(pairs, refs[-1])


def copying(kernel, prefetch, operands, outs, copies, grant=60):
    smem = [pl.BlockSpec(memory_space=pltpu.SMEM)] * len(prefetch)
    vmem = pl.BlockSpec(memory_space=pltpu.VMEM)
    return pl.pallas_call(
        kernel,
        in_specs=smem + [pl.BlockSpec(memory_space=pl.ANY)] * len(operands),
        out_specs=[vmem] * len(outs),
        out_shape=outs,
        scratch_shapes=[pltpu.SemaphoreType.DMA((copies,))],
        compiler_params=pltpu.CompilerParams(vmem_limit_bytes=grant * 2**20),
        cost_estimate=pl.CostEstimate(flops=0, bytes_accessed=0, transcendentals=0),
    )(*prefetch, *operands)


def halves(tokens):
    out = jax.ShapeDtypeStruct((tokens.shape[0] // 2, tokens.shape[1]), tokens.dtype)
    return copying(halves_kernel, (), (tokens,), [out, out], 2)


def cut(parts, place, key_matrix, value_matrix, query_matrix):
    feats, narrow = key_matrix.shape
    span = 2 * HEAD_DIM + query_matrix.shape[1] * HEAD_DIM // narrow
    outs = [jax.ShapeDtypeStruct((feats // 2 if sent else feats, span), key_matrix.dtype) for _, sent in parts]
    kernel = functools.partial(cut_kernel, parts)
    grant = 60 if len(parts) == 1 else 24
    return copying(kernel, (place,), (key_matrix, value_matrix, query_matrix), outs, 3 * len(parts), grant)


def sums_kernel(layout, begun, place_ref, *refs):
    if begun:
        weights_ref, theirs_ref, out_ref, rows_ref, feats_ref = refs[-5:]
        begun_refs = out_ref, rows_ref
    else:
        weights_ref, theirs_ref, others_ref, out_ref, feats_ref = refs[-5:]
        begun_refs = ()
    first_core, group = place_ref[1], place_ref[2]
    share, half = feats_ref.shape[1] // len(layout), theirs_ref.shape[0]
    rest = list(refs[:-5])
    for i, counts in enumerate(layout):
        start = 0 if len(layout) == 1 else (place_ref[0] if i == 0 else 1 - place_ref[0]) * share
        for block, count in zip((1 - first_core, first_core), counts):
            done = 0
            for piece_ref in [rest.pop(0) for _ in range(count)]:
                rows = pl.ds(pl.multiple_of(start + done, 32), piece_ref.shape[0])
                feats_ref[block, rows, :] = piece_ref[...]
                done += piece_ref.shape[0]
    here = pl.ds(pl.multiple_of(group * half, HEAD_DIM), half)
    there = pl.ds(pl.multiple_of((1 - group) * half, HEAD_DIM), half)
    span = out_ref.shape[1]
    step = 2 * HEAD_DIM
    if begun_refs:
        begun_refs[1][...] = feats_ref[1, :, there]
    for col in range(0, span, step):
        cols = slice(col, min(span, col + step))
        total = jnp.dot(feats_ref[0], weights_ref[:, cols], preferred_element_type=jnp.float32)
        total += jnp.dot(feats_ref[1, :, here], theirs_ref[:, cols], preferred_element_type=jnp.float32)
        if not begun_refs:
            total += jnp.dot(feats_ref[1, :, there], others_ref[:, cols], preferred_element_type=jnp.float32)
        out_ref[:, cols] = total.astype(out_ref.dtype)


def finish_kernel(begun_ref, feats_ref, others_ref, out_ref):
    total = jnp.dot(feats_ref[...], others_ref[...], preferred_element_type=jnp.float32)
    out_ref[...] = (begun_ref[...] + total).astype(out_ref.dtype)


def finish(name, begun, others, dtype):
    vmem = pl.BlockSpec(memory_space=pltpu.VMEM)
    with jax.named_scope(name):
        return pl.pallas_call(
            finish_kernel,
            in_specs=[vmem] * 3,
            out_specs=vmem,
            out_shape=jax.ShapeDtypeStruct(begun[0].shape, dtype),
            compiler_params=pltpu.CompilerParams(vmem_limit_bytes=12 * 2**20),
            cost_estimate=pl.CostEstimate(flops=0, bytes_accessed=0, transcendentals=0),
        )(*begun, others)


def sums(name, place, shares, weights, theirs, others, dtype):
    layout = [tuple(len(pieces) for pieces in share) for share in shares]
    pieces = [x for share in shares for part in share for x in part]
    rows, feats = sum(x.shape[0] for share in shares for x in share[0]), weights.shape[0]
    span, half = weights.shape[1], theirs.shape[0]
    operands = [*pieces, weights, theirs] + ([] if others is None else [others])
    vmem = pl.BlockSpec(memory_space=pltpu.VMEM)
    out = jax.ShapeDtypeStruct((rows, span), dtype)
    if others is None:
        out = [out, jax.ShapeDtypeStruct((rows, half), weights.dtype)]
    with jax.named_scope(name):
        return pl.pallas_call(
            functools.partial(sums_kernel, layout, others is None),
            in_specs=[pl.BlockSpec(memory_space=pltpu.SMEM)] + [vmem] * len(operands),
            out_specs=vmem if others is not None else [vmem] * 2,
            out_shape=out,
            scratch_shapes=[pltpu.VMEM((2, rows, feats), jnp.bfloat16)],
            compiler_params=pltpu.CompilerParams(vmem_limit_bytes=12 * 2**20),
            cost_estimate=pl.CostEstimate(flops=0, bytes_accessed=0, transcendentals=0),
        )(place, *operands)


def slot_hits(holder, row_slot, width):
    lane = lax.broadcasted_iota(jnp.int32, (row_slot.shape[0], width), 1)
    return row_slot == holder * 2 + (lane >= width // 2).astype(jnp.int32)


def held_maps(inner, maps, first, buffers, sems):
    rows = buffers.shape[1]
    copies = [pltpu.make_async_copy(x.at[pl.ds(first, rows)], buffers.at[i], sems.at[i]) for i, x in enumerate(maps)]
    for copy in copies:
        copy.start()

    def held(k):
        needed = (k,) if k < 2 else (2 * k - 2, 2 * k - 1)
        for i in needed:
            copies[i].wait()
        return buffers[k] if k < 2 else buffers[2 * k - 1 - inner]

    return held


def shrink_kernel(holder_ref, slot_ref, tok_ref, *refs):
    out_ref, buffers, sems = refs[-3:]
    width = buffers.shape[2]
    total = jnp.zeros((tok_ref.shape[0], width), jnp.float32)
    held = held_maps(holder_ref[4], refs[:-3], 0, buffers, sems)
    downs = [held(k) for k in range(4)]
    for k, down in enumerate(downs):
        product = jnp.dot(tok_ref[...], down, preferred_element_type=jnp.float32)
        total += jnp.where(slot_hits(holder_ref[k], slot_ref[...], width), product, 0.0)
    total = total[:, : width // 2] + total[:, width // 2 :]
    half = out_ref.shape[0]
    out_ref[...] = jnp.concatenate([total[:half], total[half:]], axis=1)


def expand_kernel(holder_ref, slot_ref, own_ref, cores_ref, chips_ref, both_ref, *refs):
    out_ref, buffers, sems = refs[-3:]
    width = buffers.shape[2]
    held = held_maps(holder_ref[4], refs[:-3], refs[0].shape[0] - buffers.shape[1], buffers, sems)
    low_rank = (own_ref[...] + cores_ref[...]) + (chips_ref[...] + both_ref[...])
    low_rank = low_rank.astype(jnp.bfloat16)
    halves = [low_rank[:, : width // 2], low_rank[:, width // 2 :]]
    twice = jnp.concatenate([jnp.concatenate([half, half], axis=1) for half in halves], axis=0)
    total = jnp.zeros(out_ref.shape, jnp.float32)
    for k in range(4):
        up = held(k)
        spread = jnp.where(slot_hits(holder_ref[k], slot_ref[...], width), twice, jnp.zeros_like(twice))
        total += lax.dot_general(spread, up, (((1,), (1,)), ((), ())), preferred_element_type=jnp.float32)
    out_ref[...] = total.astype(out_ref.dtype)


def adapter_call(name, kernel, shape, rows, holders, operands, maps):
    vmem = pl.BlockSpec(memory_space=pltpu.VMEM)
    with jax.named_scope(name):
        return pl.pallas_call(
            kernel,
            in_specs=[pl.BlockSpec(memory_space=pltpu.SMEM)]
            + [vmem] * len(operands)
            + [pl.BlockSpec(memory_space=pl.ANY)] * len(maps),
            out_specs=vmem,
            out_shape=shape,
            scratch_shapes=[
                pltpu.VMEM((len(maps), rows, maps[0].shape[1]), maps[0].dtype),
                pltpu.SemaphoreType.DMA((len(maps),)),
            ],
            compiler_params=pltpu.CompilerParams(vmem_limit_bytes=12 * 2**20),
            cost_estimate=pl.CostEstimate(flops=0, bytes_accessed=0, transcendentals=0),
        )(holders, *operands, *maps)


PAIRED = (4, 4, 2)
FAR = [(0, 2), (3, 1)]
INNER = [(1, 2), (2, 1), (0, 0), (3, 3)]
OUTWARD = [(1, 0), (2, 3), (0, 1), (3, 2)]


def shards_paired(
    tokens,
    query_matrix,
    key_matrix,
    value_matrix,
    query_down_maps,
    query_up_maps,
    request_lengths,
    request_adapter,
    adapter_pool_slot,
):
    pools, parts, groups = PAIRED
    tok_count, feat_count = tokens.shape
    req_count = request_lengths.shape[1]
    adapter_count = adapter_pool_slot.shape[0]
    slots_own, _, rank = query_down_maps.shape
    group, pool, part = lax.axis_index("groups"), lax.axis_index("pool"), lax.axis_index("tp")
    f32, bf16 = jnp.float32, jnp.bfloat16
    dot = functools.partial(jnp.dot, preferred_element_type=f32)
    here = part // 2 == pool // 2
    first_core = pool % 2 == part % 2
    place = jnp.stack([here.astype(jnp.int32), first_core.astype(jnp.int32), group.astype(jnp.int32), (pool % 3 > 0).astype(jnp.int32)])

    def permute(name, x, axes, pairs):
        with jax.named_scope(name):
            return lax.ppermute(x, axes, pairs)

    def chip_swap(name, x, bits=2):
        return permute(name, x, "tp", [(t, t ^ bits) for t in range(parts)])

    def core_swap(name, x):
        return chip_swap(name, x, 1)

    def after(x, *done):
        return lax.optimization_barrier((x,) + done)[0]

    kv_count = key_matrix.shape[1] // HEAD_DIM
    wide = query_matrix.shape[1] // kv_count
    in_pairs = [(i, i ^ 1) for i in range(pools)]
    replicas = [(g * pools + p, (1 - g) * pools + p) for g in range(groups) for p in range(pools)]
    matrices = key_matrix, value_matrix, query_matrix
    half_rows = tok_count // 2
    (first_send,) = cut([(0, True)], place, *matrices)
    top, bottom = halves(after(tokens, first_send))

    request = request_local(request_lengths[0], tok_count)
    slot_table = jnp.sum(
        jnp.where(
            request_adapter[:, 0][:, None] == jnp.arange(adapter_count)[None, :],
            adapter_pool_slot[None, :],
            0,
        ),
        axis=1,
        dtype=jnp.int32,
    )
    row_slot = jnp.sum(
        jnp.where(request[:, None] == jnp.arange(req_count)[None, :], slot_table[None, :], 0),
        axis=1,
        dtype=jnp.int32,
    )
    bias = request_bias(request)

    top_here = chip_swap("tokens_top", top)
    first = permute("weights_0", first_send, "pool", in_pairs)
    maps = jnp.concatenate(
        [query_down_maps[i] for i in range(slots_own)], axis=1
    ), query_up_maps.reshape(slots_own * rank, -1).T
    maps = after(jnp.concatenate(maps, axis=0), top)
    inner_maps = permute("maps_inner", maps, "pool", INNER)
    leaving = jnp.where(here, after(top_here, maps, row_slot, bias), bottom)
    far = permute("tokens_far", leaving, "pool", FAR)
    later = [(kv, True) for kv in range(1, kv_count)] + [(kv, False) for kv in range(kv_count)]
    send, *weights = cut(later, after(place, leaving), *matrices)
    near = permute("tokens_near", after(leaving, far), "pool", INNER)

    pair_maps = permute("maps_pair", after(maps, first), "pool", in_pairs)
    bottom_here = chip_swap("tokens_bottom", after(bottom, leaving))
    mine = jnp.where(here, tokens, jnp.concatenate([top_here, bottom_here], axis=0))
    own_cores = core_swap("own_cores", mine)
    others = [permute("weights_0_replicas", after(first, send, *weights, inner_maps), ("groups", "pool"), replicas)]
    theirs = [first, permute("weights_1", after(send, pair_maps), "pool", in_pairs)]
    others.append(permute("weights_1_replicas", theirs[1], ("groups", "pool"), replicas))
    far_chips = chip_swap("far_chips", after(far, bottom_here))
    outer_maps = permute("maps_outer", pair_maps, "pool", INNER)
    far_cores = core_swap("far_cores_a", far), core_swap("far_cores_b", after(far_chips, others[0], pair_maps, own_cores))
    far_pieces = [([far], far_cores[:1]), ([far_chips], far_cores[1:])]
    near_chips = chip_swap("near_chips", after(near, far_chips))
    inner_out = permute("maps_inner_out", after(inner_maps, theirs[1]), "pool", OUTWARD)
    outer_out = permute("maps_outer_out", after(outer_maps, theirs[1]), "pool", OUTWARD)
    def part_sums(name, kv, pieces, dtype, earlier=()):
        both = weights[kv], theirs[kv], others[kv]
        return sums(f"{name}_{kv}", after(place, *earlier), pieces, *both, dtype)

    far_0 = part_sums("far", 0, far_pieces, bf16)
    arrived_far = [permute("sums_far_0", far_0, "pool", INNER)]
    near_cores = core_swap("near_cores_a", near)
    fine = half_rows // 2
    near_fine = [core_swap(f"near_cores_b{i}", near_chips[i * fine : (i + 1) * fine]) for i in range(2)]
    near_pieces = [([near], [near_cores]), ([near_chips], near_fine)]
    near_0 = part_sums("near", 0, near_pieces, bf16, (far_0, outer_maps))
    arrived_near = [permute("sums_near_0", after(near_0, arrived_far[0]), "pool", INNER)]
    own_pieces = [([mine], [own_cores])]
    own_0 = part_sums("own", 0, own_pieces, f32, (near_0,))
    begun = sums("far_1_begun", after(place, near_0), far_pieces, weights[1], theirs[1], None, f32)
    far_1 = finish("far_1", begun, after(others[1], own_0, inner_out), bf16)
    arrived_far.append(permute("sums_far_1", after(far_1, arrived_near[0], arrived_far[0]), "pool", INNER))
    forwarded = [permute("sums_out_0", arrived_far[0], "pool", OUTWARD)]
    own = [own_0, part_sums("own", 1, own_pieces, f32, (far_1,))]

    inner = 2 - pool // 2
    holders = jnp.stack([pool, pool ^ 1, inner, inner ^ 1, place[3]]).astype(jnp.int32)
    held = maps, pair_maps, inner_maps, inner_out, outer_maps, outer_out
    slots = row_slot[:, None]
    shrunk = jax.ShapeDtypeStruct((half_rows, 2 * rank), f32)
    shrunk = adapter_call(
        "low_rank", shrink_kernel, shrunk, feat_count, holders, (slots, after(tokens, near_0)), held
    )
    shares = [shrunk] + [chip_swap(f"low_rank_{bits}", shrunk, bits) for bits in range(1, parts)]
    near_1 = part_sums("near", 1, near_pieces, bf16, (shrunk,))
    arrived_near.append(permute("sums_near_1", after(near_1, arrived_far[1]), "pool", INNER))
    forwarded.append(permute("sums_out_1", arrived_far[1], "pool", OUTWARD))
    delta = jax.ShapeDtypeStruct((tok_count, query_matrix.shape[1]), bf16)
    delta = adapter_call(
        "delta", expand_kernel, delta, maps.shape[0] - feat_count, after(holders, own[1], forwarded[0]), (slots, *shares), held
    )
    mixed = None
    for kv in range(kv_count):
        mixed = attend_head(kv, kv_count, place, own[kv], arrived_near[kv], forwarded[kv], delta, bias, mixed)
    return mixed


def solution(mesh):
    placed = (
        P(("groups", "pool"), "tp"),
        P("pool", "tp"),
        P("pool", "tp"),
        P("pool", "tp"),
        P(("groups", "pool"), "tp", None),
        P(("groups", "pool"), None, "tp"),
        P(("groups", "pool"), None),
        P(("groups", "pool"), None),
        P(),
    )
    sizes = mesh.shape
    if (sizes["pool"], sizes["tp"], sizes["groups"]) == PAIRED:
        shards = shards_paired
    else:
        shards = shards_gathered
    return jax.shard_map(
        shards, mesh=mesh, in_specs=placed, out_specs=P(("groups", "pool"), "tp"), check_vma=False
    )
```
